512 devices in a mesh: dp: 8 (over y, core), fsdp: 64 (over x, z).
Axes of the slice: x: 4, y: 4, z: 16, core: 2. Of those that a mesh axis runs over, the one named last changes fastest.
Arguments:
- grads: bfloat16 [8, 64, 2048, 768], P('dp', None, 'fsdp'), as said below
- momentum: float32 [64, 2048, 768], P(None, ('fsdp', 'dp')), as said below
- slot_matrix: int32 [64], replicated, may hold values from 0 to 63, each once
Outputs:
- update: bfloat16 [64, 2048, 768], P(None, ('fsdp', 'dp'))
- new_momentum: float32 [64, 2048, 768], P(None, ('fsdp', 'dp'))
The draws below stay inside these ranges and needn't reach their ends.
Inputs may be any that keep to these rules, and one draw needn't show every extreme that they name: `slot_matrix`: every matrix index appears in exactly one slot. `grads`: finite values. `momentum`: finite values.
All inputs are finite; a program needn't handle non-finite values.
Results may differ from the reference program's by a relative error of at most 0.025.
Values may be sent and summed in bfloat16 or wider, within the bound.
No kernel may reach another device: no remote copies, remote signals or barrier semaphores. Data moves between devices by JAX's collectives and lax.ppermute only.
A program may use at most 64 MiB of HBM per device.

```python
import math
import jax
import jax.numpy as jnp
from jax import lax

R = 2048
C = 768
ITERS = 2
M = 64
N_DP = 8


def spread_scales(key, top):
    row_key, col_key = jax.random.split(key)
    row_scale = jnp.exp(jax.random.uniform(row_key, (R,), jnp.float32, 0.0, math.log(top)))
    col_scale = jnp.exp(jax.random.uniform(col_key, (C,), jnp.float32, 0.0, math.log(top)))
    return (row_scale, col_scale)


def shared_pattern(key):
    key = jax.random.fold_in(key, 7)
    left_key, right_key = jax.random.split(key)
    left_vecs = jax.random.normal(left_key, (2, M, R), jnp.float32)
    right_vecs = jax.random.normal(right_key, (2, M, C), jnp.float32)
    first = left_vecs[0][:, :, None] * right_vecs[0][:, None, :]
    second = left_vecs[1][:, :, None] * right_vecs[1][:, None, :]
    return (first + 0.6 * second) * 0.857


def draw_grads(key, part):
    pattern = shared_pattern(key)
    row_scale, col_scale = spread_scales(key, 10.0)
    key = jax.random.fold_in(key, 11)
    noise = jax.random.normal(key, (N_DP, M, R, C), jnp.float32) * 0.1
    values = noise + 0.1 / math.sqrt(N_DP) * pattern[None]
    values = values * row_scale[:, None] * col_scale[None, :]
    return values.astype(jnp.bfloat16)


def draw_momentum(key, part):
    pattern = shared_pattern(key)
    row_scale, col_scale = spread_scales(key, 10.0)
    key = jax.random.fold_in(key, 12)
    values = jax.random.normal(key, (M, R, C), jnp.float32) * 0.3 + 0.3 * pattern
    return values * row_scale[:, None] * col_scale[None, :]


def setup_inputs(seed: int = 0) -> dict:
    key_list = jax.random.split(jax.random.key(seed), 4)
    grads = draw_grads(jax.random.fold_in(key_list[3], 71), 0)
    momentum = draw_momentum(jax.random.fold_in(key_list[3], 71), 0)
    slot_matrix = jax.random.permutation(key_list[2], M).astype(jnp.int32)
    return {"grads": grads, "momentum": momentum, "slot_matrix": slot_matrix}


coef_one = 3.4445
coef_two = -4.775
coef_three = 2.0315
decay_rate = 0.95

def polish(gram_total):
    trace_sum = jnp.trace(gram_total)
    inv_norm = 1.0 / (jnp.sqrt(trace_sum) + 1e-07)
    level_now = gram_total * inv_norm * inv_norm
    identity = jnp.eye(gram_total.shape[0], dtype=jnp.float32)
    total_now = None
    for step in range(ITERS):
        level_low = level_now.astype(jnp.bfloat16)
        square = jnp.dot(level_low, level_low, preferred_element_type=jnp.float32)
        poly_now = coef_one * identity + coef_two * level_now + coef_three * square
        poly_low = poly_now.astype(jnp.bfloat16)
        if step == 0:
            total_now = poly_now
        else:
            total_now = jnp.dot(total_now.astype(jnp.bfloat16), poly_low, preferred_element_type=jnp.float32)
        if step + 1 < ITERS:
            left_half = jnp.dot(poly_low, level_low, preferred_element_type=jnp.float32).astype(jnp.bfloat16)
            level_now = jnp.dot(left_half, poly_low, preferred_element_type=jnp.float32)
    return (inv_norm, total_now.astype(jnp.bfloat16))

def one_matrix(nesterov):
    gram_total = jnp.dot(nesterov.T, nesterov, preferred_element_type=jnp.float32)
    inv_norm, total_low = polish(gram_total)
    factor = jnp.sqrt(jnp.float32(max(R, C))) * inv_norm
    product = jnp.dot(nesterov, total_low, preferred_element_type=jnp.float32)
    return (product * factor).astype(jnp.bfloat16)

def reference(grads, momentum, slot_matrix):
    summed = jnp.zeros((M, R, C), jnp.float32)
    for replica in range(N_DP):
        summed = summed + grads[replica].astype(jnp.float32)
    gradient = jnp.zeros((M, R, C), jnp.float32).at[slot_matrix.astype(jnp.int32)].set(summed)
    new_momentum = decay_rate * momentum + gradient
    nesterov = (gradient + decay_rate * new_momentum).astype(jnp.bfloat16)
    update = lax.map(one_matrix, nesterov)
    return (update, new_momentum)
```

```python
import functools
import math

import jax
import jax.numpy as jnp
from jax import lax
from jax.experimental import pallas as pl
from jax.experimental.pallas import tpu as pltpu
from jax.sharding import PartitionSpec as P

NY = 4
NX = 4
COEF_A = 3.4445
COEF_B = -4.775
COEF_C = 2.0315
DECAY = 0.95
BF = jnp.bfloat16
F32 = jnp.float32
SMEM = pltpu.SMEM


def sds(shape, dtype):
    return jax.ShapeDtypeStruct(shape, dtype)


def params(mib=16):
    return pltpu.CompilerParams(vmem_limit_bytes=mib * 1024 * 1024)


def whole(n):
    return [pl.BlockSpec(memory_space=pltpu.VMEM)] * n


def split_kernel(pos, g_ref, send2, send013, keep2, keep013, scr):
    y = pos[0]
    c = pos[1]
    scr[...] = g_ref[0].astype(F32)

    def emit(low):
        slot = 0
        for rel in range(NY):
            yy = lax.rem(y + rel, NY)
            both = scr[:, pl.ds(pl.multiple_of(8 * yy, 8), 8), :]
            own = both[:, 4 * low : 4 * low + 4, :].astype(BF)
            other = both[:, 4 - 4 * low : 8 - 4 * low, :].astype(BF)
            if rel == 2:
                send2[...] = other
                keep2[...] = own
            else:
                send013[slot] = other
                keep013[slot] = own
                slot += 1

    pl.when(c == 0)(lambda: emit(0))
    pl.when(c == 1)(lambda: emit(1))


def split_rows(pos, grads, mb):
    _, m, rows, cols = grads.shape
    one = pl.BlockSpec((mb, 4, cols), lambda i: (i, 0, 0))
    three = pl.BlockSpec((3, mb, 4, cols), lambda i: (0, i, 0, 0))
    return pl.pallas_call(
        split_kernel,
        grid=(m // mb,),
        in_specs=[
            pl.BlockSpec(memory_space=SMEM),
            pl.BlockSpec((1, mb, rows, cols), lambda i: (0, i, 0, 0)),
        ],
        out_specs=[one, three, one, three],
        out_shape=[
            sds((m, 4, cols), BF),
            sds((3, m, 4, cols), BF),
            sds((m, 4, cols), BF),
            sds((3, m, 4, cols), BF),
        ],
        scratch_shapes=[pltpu.VMEM((mb, rows, cols), F32)],
        compiler_params=params(),
        name="split_rows",
    )(pos, grads)


def momentum_kernel(nz, pos, slots, own, dir_a, rel_a, dir_b, rel_b, mom, n0, n1, n2, n3, new_mom, total, inv):
    x = pos[2]
    m = mom.shape[0]
    h = m // 2

    def invert(j, carry):
        inv[slots[j]] = j
        return carry

    lax.fori_loop(0, m, invert, 0)

    def add_up(j, carry):
        total[j] = own[j] + dir_a[j].astype(F32) + rel_a[j].astype(F32)
        total[h + j] = own[h + j] + dir_b[j].astype(F32) + rel_b[j].astype(F32)
        return carry

    lax.fori_loop(0, h, add_up, 0, unroll=min(4, h))
    for rel, out in enumerate((n0, n1, n2, n3)):
        base = lax.rem(x + rel, NX) * nz

        def step(z, carry, out=out, base=base):
            mat = base + z
            gradient = total[inv[mat]]
            new = DECAY * mom[mat] + gradient
            new_mom[mat] = new
            out[z] = (gradient + DECAY * new).astype(BF)
            return carry

        lax.fori_loop(0, nz, step, 0, unroll=min(4, nz))


def momentum_step(nz, pos, slots, own, dir_a, rel_a, dir_b, rel_b, mom):
    m, _, cols = mom.shape
    return pl.pallas_call(
        functools.partial(momentum_kernel, nz),
        in_specs=[pl.BlockSpec(memory_space=SMEM)] * 2 + whole(6),
        out_specs=whole(5),
        out_shape=[sds((nz, 4, cols), BF)] * 4 + [sds((m, 4, cols), F32)],
        scratch_shapes=[pltpu.VMEM((m, 4, cols), F32), pltpu.SMEM((m,), jnp.int32)],
        compiler_params=params(),
        name="momentum_step",
    )(pos, slots, own, dir_a, rel_a, dir_b, rel_b, mom)


def pack_z_kernel(a0, a1, a2, a3, out):
    nz = a0.shape[0]
    for rel, ref in enumerate((a0, a1, a2, a3)):
        for z in range(nz):
            out[NX * z + rel] = ref[z]


def pack_z(parts):
    nz, _, cols = parts[0].shape
    return pl.pallas_call(
        pack_z_kernel,
        in_specs=whole(4),
        out_specs=whole(1)[0],
        out_shape=sds((NX * nz, 4, cols), BF),
        compiler_params=params(),
        name="pack_z",
    )(*parts)


def pack_x_kernel(*refs):
    ins, outs = refs[:-4], refs[-4:]
    for rel, out in enumerate(outs):
        for k, ref in enumerate(ins):
            out[k] = ref[rel]


def pack_x(parts):
    nz = len(parts)
    cols = parts[0].shape[2]
    return pl.pallas_call(
        pack_x_kernel,
        in_specs=whole(nz),
        out_specs=whole(4),
        out_shape=[sds((nz, 4, cols), BF)] * 4,
        compiler_params=params(),
        name="pack_x",
    )(*parts)


def place_kernel(pos, q0, q1, q2, q3, out):
    x = pos[2]
    z = pos[3]
    nz = q0.shape[0]
    for rel, ref in enumerate((q0, q1, q2, q3)):
        base = lax.rem(x + rel, NX) * nz
        for k in range(nz):
            out[base + lax.rem(z - k + nz, nz)] = ref[k]


def place(pos, parts):
    nz, _, cols = parts[0].shape
    return pl.pallas_call(
        place_kernel,
        in_specs=[pl.BlockSpec(memory_space=SMEM)] + whole(4),
        out_specs=whole(1)[0],
        out_shape=sds((NX * nz, 4, cols), BF),
        compiler_params=params(),
        name="place",
    )(pos, *parts)


def blocks_of(cols):
    n = cols // 128
    return [(i, j) for i in range(n) for j in range(i, n)]


def gram_kernel(pos, a_ref, rows_ref, send, keep, slabs):
    c = pos[1]
    count, _, cols = a_ref.shape
    for g in range(count // 4):
        four = [a_ref[4 * g + i].astype(F32) for i in range(4)]
        rows_ref[16 * g : 16 * g + 16, :] = jnp.concatenate(four, axis=0).astype(BF)
    n = cols // 128
    b = 0
    for i in range(n):
        strip = lax.dot_general(
            rows_ref[:, 128 * i : 128 * i + 128],
            rows_ref[:, 128 * i :],
            (((0,), (0,)), ((), ())),
            preferred_element_type=F32,
        )
        for j in range(i, n):
            block = strip[:, 128 * (j - i) : 128 * (j - i) + 128]
            for q in range(4):
                slabs[q, b] = block[32 * q : 32 * q + 32, :]
            b += 1
    send[...] = slabs[pl.ds(2 * (1 - c), 2)].astype(BF)
    keep[...] = slabs[pl.ds(2 * c, 2)]


def partial_gram(pos, a):
    count, _, cols = a.shape
    nb = len(blocks_of(cols))
    return pl.pallas_call(
        gram_kernel,
        in_specs=[pl.BlockSpec(memory_space=SMEM)] + whole(1),
        out_specs=whole(3),
        out_shape=[
            sds((4 * count, cols), BF),
            sds((2, nb, 32, 128), BF),
            sds((2, nb, 32, 128), F32),
        ],
        scratch_shapes=[pltpu.VMEM((4, nb, 32, 128), F32)],
        compiler_params=params(),
        name="partial_gram",
    )(pos, a)


def polish_kernel(nz, scale, pos, own, other, rows_ref, *rest):
    outs = rest[:nz]
    slabs, level, low, poly, high, result = rest[nz:]
    c = pos[1]
    z = pos[3]
    count, cols = rows_ref.shape
    n = cols // 128
    slabs[pl.ds(2 * c, 2)] = own[...].astype(F32)
    slabs[pl.ds(2 * (1 - c), 2)] = other[...].astype(F32)

    eye = (
        lax.broadcasted_iota(jnp.int32, (128, 128), 0) == lax.broadcasted_iota(jnp.int32, (128, 128), 1)
    )
    diag = jnp.zeros((128, 128), F32)
    for b, (i, j) in enumerate(blocks_of(cols)):
        if i == j:
            diag += slabs[:, b].reshape(128, 128)
    trace = jnp.sum(jnp.where(eye, diag, 0.0))
    inv_norm = 1.0 / (jnp.sqrt(jnp.full((1, 1), trace)) + 1e-7)
    square = inv_norm * inv_norm
    for b, (i, j) in enumerate(blocks_of(cols)):
        block = slabs[:, b].reshape(128, 128) * square
        level[128 * i : 128 * i + 128, 128 * j : 128 * j + 128] = block
        low[128 * i : 128 * i + 128, 128 * j : 128 * j + 128] = block.astype(BF)
        if i != j:
            block = block.T
            level[128 * j : 128 * j + 128, 128 * i : 128 * i + 128] = block
            low[128 * j : 128 * j + 128, 128 * i : 128 * i + 128] = block.astype(BF)

    step = 256 if cols % 256 == 0 else 128
    for r in range(0, cols, step):
        part = jnp.dot(low[r : r + step, :], low[...], preferred_element_type=F32)
        poly[r : r + step, :] = (COEF_B * level[r : r + step, :] + COEF_C * part).astype(BF)
    for r in range(0, cols, step):
        part = jnp.dot(poly[r : r + step, :], low[...], preferred_element_type=F32)
        left_now = COEF_A * level[r : r + step, :] + part
        left_low = left_now.astype(BF)
        high[r : r + step, :] = (
            COEF_A * left_now + jnp.dot(left_low, poly[...], preferred_element_type=F32)
        ).astype(BF)
    rows = rows_ref[...]
    y0 = COEF_A * rows.astype(F32) + jnp.dot(rows, poly[...], preferred_element_type=F32)
    result[...] = COEF_A * y0
    y1 = jnp.dot(y0.astype(BF), high[...], preferred_element_type=F32)
    result[...] += COEF_B * y1
    y2 = jnp.dot(y1.astype(BF), high[...], preferred_element_type=F32)
    result[...] = (result[...] + COEF_C * y2) * (scale * inv_norm)
    for k in range(nz):
        start = pl.multiple_of(16 * lax.rem(z + k, nz), 16)
        group = result[pl.ds(start, 16), :]
        for i in range(4):
            outs[k][i] = group[4 * i : 4 * i + 4, :].astype(BF)


def polish(nz, scale, pos, own, other, rows):
    count, cols = rows.shape
    nb = own.shape[1]
    return pl.pallas_call(
        functools.partial(polish_kernel, nz, scale),
        in_specs=[pl.BlockSpec(memory_space=SMEM)] + whole(3),
        out_specs=whole(nz),
        out_shape=[sds((4, 4, cols), BF)] * nz,
        scratch_shapes=[
            pltpu.VMEM((4, nb, 32, 128), F32),
            pltpu.VMEM((cols, cols), F32),
            pltpu.VMEM((cols, cols), BF),
            pltpu.VMEM((cols, cols), BF),
            pltpu.VMEM((cols, cols), BF),
            pltpu.VMEM((count, cols), F32),
        ],
        compiler_params=params(32),
        name="polish",
    )(pos, own, other, rows)


def shards(n_rows, grads, momentum, slot_matrix):
    m = grads.shape[1]
    cols = grads.shape[3]
    nf = m
    nz = nf // NX
    d = lax.axis_index("dp")
    f = lax.axis_index("fsdp")
    pos = jnp.stack([d // 2, d % 2, f // nz, f % nz]).astype(jnp.int32)
    h = m // 2

    def core_swap(v):
        return lax.ppermute(v, "dp", [(i, i ^ 1) for i in range(2 * NY)])

    def y_shift(v, by):
        return lax.ppermute(v, "dp", [(i, (i + 2 * by) % (2 * NY)) for i in range(2 * NY)])

    def y_pair(v, odd):
        perm = []
        for y in range(NY):
            to = (y ^ 1) if not odd else ((y + 1) % NY if y % 2 else (y - 1) % NY)
            perm += [(2 * y, 2 * to), (2 * y + 1, 2 * to + 1)]
        return lax.ppermute(v, "dp", perm)

    def x_shift(v, by):
        return lax.ppermute(v, "fsdp", [(i, (i + nz * by) % nf) for i in range(nf)])

    def z_shift(v, by):
        return lax.ppermute(v, "fsdp", [(i, i // nz * nz + (i % nz + by) % nz) for i in range(nf)])

    send2, send013, keep2, keep013 = split_rows(pos, grads, min(8, m))
    sum2 = keep2.astype(F32) + core_swap(send2).astype(F32)
    sum2 = sum2.astype(BF)
    relay_a = y_shift(sum2[:h], 1)
    relay_b = y_shift(sum2[h:], -1)
    sums = keep013.astype(F32) + core_swap(send013).astype(F32)
    dir_b = y_shift(sums[1, h:].astype(BF), 1)
    dir_a = y_shift(sums[2, :h].astype(BF), -1)
    rel_a = y_shift((sums[1, :h] + relay_a.astype(F32)).astype(BF), 1)
    rel_b = y_shift((sums[2, h:] + relay_b.astype(F32)).astype(BF), -1)
    parts = momentum_step(nz, pos, slot_matrix, sums[0], dir_a, rel_a, dir_b, rel_b, momentum)
    new_momentum = parts[4]

    arrived = [parts[0]] + [x_shift(parts[rel], rel) for rel in range(1, NX)]
    groups = [[nz * x + z for z in range(nz)] for x in range(NX)]
    mine = lax.all_to_all(
        pack_z(arrived), "fsdp", split_axis=0, concat_axis=0, axis_index_groups=groups, tiled=True
    )

    rows, gram_send, gram_keep = partial_gram(pos, mine)
    gram = gram_keep + core_swap(gram_send).astype(F32)
    one, two = gram[0], gram[1]
    one_in, two_in = y_pair(one.astype(BF), False), y_pair(two.astype(BF), True)
    one = one + one_in.astype(F32)
    two = two + two_in.astype(F32)
    one_in, two_in = y_pair(one.astype(BF), True), y_pair(two.astype(BF), False)
    one = one + one_in.astype(F32)
    two = two + two_in.astype(F32)
    own = jnp.stack([one, two]).astype(BF)
    other = core_swap(own)

    pieces = polish(nz, math.sqrt(max(n_rows, cols)), pos, own, other, rows)
    back = [pieces[0]] + [z_shift(pieces[k], k) for k in range(1, nz)]
    packed = pack_x(back)
    home = [packed[0]] + [x_shift(packed[rel], -rel) for rel in range(1, NX)]
    return (place(pos, home), new_momentum)


def solution(mesh):
    in_specs = (P("dp", None, "fsdp", None), P(None, ("fsdp", "dp"), None), P())
    out_specs = (P(None, ("fsdp", "dp"), None), P(None, ("fsdp", "dp"), None))

    def run(grads, momentum, slot_matrix):
        body = functools.partial(shards, grads.shape[2])
        return jax.shard_map(body, mesh=mesh, in_specs=in_specs, out_specs=out_specs, check_vma=False)(
            grads, momentum, slot_matrix
        )

    return run
```

```python
import functools
import math

import jax
import jax.numpy as jnp
from jax import lax
from jax.experimental import pallas as pl
from jax.experimental.pallas import tpu as pltpu
from jax.sharding import PartitionSpec as P

NY = 4
COEF_A = 3.4445
COEF_B = -4.775
COEF_C = 2.0315
DECAY = 0.95
BF = jnp.bfloat16
F32 = jnp.float32
SMEM = pltpu.SMEM


def sds(shape, dtype):
    return jax.ShapeDtypeStruct(shape, dtype)


def params(mib=16):
    return pltpu.CompilerParams(vmem_limit_bytes=mib * 1024 * 1024)


def whole(n):
    return [pl.BlockSpec(memory_space=pltpu.VMEM)] * n


def place_of():
    d = lax.axis_index("dp")
    y, c = lax.div(d, 2), lax.rem(d, 2)
    flip, turn = y + 1 - 2 * lax.rem(y, 2), NY - 1 - y
    near = jnp.where(c == 0, flip, turn)
    far = jnp.where(c == 0, turn, flip)
    return y, c, near, far, lax.rem(y + 2, NY)


def split_kernel(g_ref, send_a, send_b, keep_a, keep_b, scr):
    y, c, near, far, across = place_of()
    scr[...] = g_ref[0].astype(F32)

    def emit(low):
        def rows(yy, core):
            both = scr[:, pl.ds(pl.multiple_of(8 * yy, 8), 8), :]
            return both[:, 4 * core : 4 * core + 4, :].astype(BF)

        send_a[0] = rows(far, 1 - low)
        send_a[1] = rows(across, 1 - low)
        send_b[0] = rows(y, 1 - low)
        send_b[1] = rows(near, 1 - low)
        keep_a[0] = rows(near, low)
        keep_a[1] = rows(across, low)
        keep_b[0] = rows(y, low)
        keep_b[1] = rows(far, low)

    pl.when(c == 0)(lambda: emit(0))
    pl.when(c == 1)(lambda: emit(1))


def split_rows(grads, mb):
    _, m, rows, cols = grads.shape
    two = pl.BlockSpec((2, mb, 4, cols), lambda i: (0, i, 0, 0))
    return pl.pallas_call(
        split_kernel,
        grid=(m // mb,),
        in_specs=[pl.BlockSpec((1, mb, rows, cols), lambda i: (0, i, 0, 0))],
        out_specs=[two] * 4,
        out_shape=[sds((2, m, 4, cols), BF)] * 4,
        scratch_shapes=[pltpu.VMEM((mb, rows, cols), F32)],
        compiler_params=params(),
        name="split_rows",
    )(grads)


def momentum_kernel(slots, keep, swapped, first, second, mom, nesterov, new_mom):
    m = mom.shape[0]

    def step(j, carry):
        mat = slots[j]
        gradient = (keep[0, j].astype(F32) + swapped[0, j].astype(F32)) + (
            first[0, j].astype(F32) + second[j].astype(F32)
        )
        new = DECAY * mom[mat] + gradient
        new_mom[mat] = new
        nesterov[mat] = (gradient + DECAY * new).astype(BF)
        return carry

    lax.fori_loop(0, m, step, 0, unroll=min(8, m))


def momentum_step(slots, keep, swapped, first, second, mom):
    m, _, cols = mom.shape
    return pl.pallas_call(
        momentum_kernel,
        in_specs=[pl.BlockSpec(memory_space=SMEM)] + whole(5),
        out_specs=whole(2),
        out_shape=[sds((m, 4, cols), BF), sds((m, 4, cols), F32)],
        compiler_params=params(),
        name="momentum_step",
    )(slots, keep, swapped, first, second, mom)


def blocks_of(cols):
    n = cols // 128
    return [(i, j) for i in range(n) for j in range(i, n)]


def gram_kernel(a_ref, rows_ref, send, keep, slabs):
    c = lax.rem(lax.axis_index("dp"), 2)
    count, _, cols = a_ref.shape
    for g in range(count // 4):
        four = [a_ref[4 * g + i].astype(F32) for i in range(4)]
        rows_ref[16 * g : 16 * g + 16, :] = jnp.concatenate(four, axis=0).astype(BF)
    n = cols // 128
    b = 0
    for i in range(n):
        strip = lax.dot_general(
            rows_ref[:, 128 * i : 128 * i + 128],
            rows_ref[:, 128 * i :],
            (((0,), (0,)), ((), ())),
            preferred_element_type=F32,
        )
        for j in range(i, n):
            block = strip[:, 128 * (j - i) : 128 * (j - i) + 128]
            slabs[0, b] = block[:64, :]
            slabs[1, b] = block[64:, :]
            b += 1
    send[...] = slabs[1 - c].astype(BF)
    keep[...] = slabs[c]


def partial_gram(a):
    count, _, cols = a.shape
    nb = len(blocks_of(cols))
    return pl.pallas_call(
        gram_kernel,
        in_specs=whole(1),
        out_specs=whole(3),
        out_shape=[
            sds((4 * count, cols), BF),
            sds((nb, 64, 128), BF),
            sds((nb, 64, 128), F32),
        ],
        scratch_shapes=[pltpu.VMEM((2, nb, 64, 128), F32)],
        compiler_params=params(),
        name="partial_gram",
    )(a)


def polish_kernel(scale, own, other, rows_ref, out, slabs, level, low, poly, high):
    c = lax.rem(lax.axis_index("dp"), 2)
    count, cols = rows_ref.shape
    n = cols // 128
    slabs[c] = own[...].astype(F32)
    slabs[1 - c] = other[...].astype(F32)

    eye = (
        lax.broadcasted_iota(jnp.int32, (128, 128), 0) == lax.broadcasted_iota(jnp.int32, (128, 128), 1)
    )
    diag = jnp.zeros((128, 128), F32)
    for b, (i, j) in enumerate(blocks_of(cols)):
        if i == j:
            diag += slabs[:, b].reshape(128, 128)
    trace = jnp.sum(jnp.where(eye, diag, 0.0))
    inv_norm = 1.0 / (jnp.sqrt(jnp.full((1, 1), trace)) + 1e-7)
    square = inv_norm * inv_norm
    for b, (i, j) in enumerate(blocks_of(cols)):
        block = slabs[:, b].reshape(128, 128) * square
        level[128 * i : 128 * i + 128, 128 * j : 128 * j + 128] = block
        low[128 * i : 128 * i + 128, 128 * j : 128 * j + 128] = block.astype(BF)
        if i != j:
            block = block.T
            level[128 * j : 128 * j + 128, 128 * i : 128 * i + 128] = block
            low[128 * j : 128 * j + 128, 128 * i : 128 * i + 128] = block.astype(BF)

    step = 256 if cols % 256 == 0 else 128
    for r in range(0, cols, step):
        part = jnp.dot(low[r : r + step, :], low[...], preferred_element_type=F32)
        poly[r : r + step, :] = (COEF_B * level[r : r + step, :] + COEF_C * part).astype(BF)
    for r in range(0, cols, step):
        part = jnp.dot(poly[r : r + step, :], low[...], preferred_element_type=F32)
        left_now = COEF_A * level[r : r + step, :] + part
        left_low = left_now.astype(BF)
        high[r : r + step, :] = (
            COEF_A * left_now + jnp.dot(left_low, poly[...], preferred_element_type=F32)
        ).astype(BF)
    rows = rows_ref[...]
    y0 = COEF_A * rows.astype(F32) + jnp.dot(rows, poly[...], preferred_element_type=F32)
    y1 = jnp.dot(y0.astype(BF), high[...], preferred_element_type=F32)
    y2 = jnp.dot(y1.astype(BF), high[...], preferred_element_type=F32)
    result = (COEF_A * y0 + COEF_B * y1 + COEF_C * y2) * (scale * inv_norm)
    for i in range(count // 4):
        out[i] = result[4 * i : 4 * i + 4, :].astype(BF)


def polish(scale, own, other, rows):
    count, cols = rows.shape
    nb = own.shape[0]
    return pl.pallas_call(
        functools.partial(polish_kernel, scale),
        in_specs=whole(3),
        out_specs=whole(1)[0],
        out_shape=sds((count // 4, 4, cols), BF),
        scratch_shapes=[
            pltpu.VMEM((2, nb, 64, 128), F32),
            pltpu.VMEM((cols, cols), F32),
            pltpu.VMEM((cols, cols), BF),
            pltpu.VMEM((cols, cols), BF),
            pltpu.VMEM((cols, cols), BF),
        ],
        compiler_params=params(32),
        name="polish",
    )(own, other, rows)


def core_swap(v):
    return lax.ppermute(v, "dp", [(i, i ^ 1) for i in range(2 * NY)])


def y_swap(v, second):
    perm = []
    for y in range(NY):
        for c in range(2):
            to = (y ^ 1) if c == second else NY - 1 - y
            perm.append((2 * y + c, 2 * to + c))
    return lax.ppermute(v, "dp", perm)


def shards(n_rows, grads, momentum, slot_matrix):
    m = grads.shape[1]
    cols = grads.shape[3]

    send_a, send_b, keep_a, keep_b = split_rows(grads, min(8, m))
    swapped_a = core_swap(send_a)
    swapped_b = core_swap(send_b)
    first = y_swap((keep_a.astype(F32) + swapped_a.astype(F32)).astype(BF), 0)
    far = (keep_b[1].astype(F32) + swapped_b[1].astype(F32)) + first[1].astype(F32)
    second = y_swap(far.astype(BF), 1)
    nesterov, new_momentum = momentum_step(slot_matrix, keep_b, swapped_b, first, second, momentum)

    mine = lax.all_to_all(nesterov, "fsdp", split_axis=0, concat_axis=0, tiled=True)

    rows, gram_send, gram_keep = partial_gram(mine)
    gram = gram_keep + core_swap(gram_send).astype(F32)
    gram = gram + y_swap(gram.astype(BF), 0).astype(F32)
    gram = gram + y_swap(gram.astype(BF), 1).astype(F32)
    own = gram.astype(BF)
    other = core_swap(own)

    update = polish(math.sqrt(max(n_rows, cols)), own, other, rows)
    update = lax.all_to_all(update, "fsdp", split_axis=0, concat_axis=0, tiled=True)
    return (update, new_momentum)


def solution(mesh):
    in_specs = (P("dp", None, "fsdp", None), P(None, ("fsdp", "dp"), None), P())
    out_specs = (P(None, ("fsdp", "dp"), None), P(None, ("fsdp", "dp"), None))

    def run(grads, momentum, slot_matrix):
        body = functools.partial(shards, grads.shape[2])
        return jax.shard_map(body, mesh=mesh, in_specs=in_specs, out_specs=out_specs, check_vma=False)(
            grads, momentum, slot_matrix
        )

    return run
```

```python
import functools
import math

import jax
import jax.numpy as jnp
from jax import lax
from jax.experimental import pallas as pl
from jax.experimental.pallas import tpu as pltpu
from jax.sharding import PartitionSpec as P

NY = 4
COEF_A = 3.4445
COEF_B = -4.775
COEF_C = 2.0315
DECAY = 0.95
BF = jnp.bfloat16
F32 = jnp.float32
SMEM = pltpu.SMEM


def sds(shape, dtype):
    return jax.ShapeDtypeStruct(shape, dtype)


def params(mib=16):
    return pltpu.CompilerParams(vmem_limit_bytes=mib * 1024 * 1024)


def whole(n):
    return [pl.BlockSpec(memory_space=pltpu.VMEM)] * n


def place_of():
    d = lax.axis_index("dp")
    y, c = lax.div(d, 2), lax.rem(d, 2)
    flip, turn = y + 1 - 2 * lax.rem(y, 2), NY - 1 - y
    near = jnp.where(c == 0, flip, turn)
    far = jnp.where(c == 0, turn, flip)
    return y, c, near, far, lax.rem(y + 2, NY)


def split_kernel(g_ref, send_a, send_b, keep_a, keep_b, scr):
    y, c, near, far, across = place_of()
    scr[...] = g_ref[0].astype(F32)

    def emit(low):
        def rows(yy, core):
            both = scr[:, pl.ds(pl.multiple_of(8 * yy, 8), 8), :]
            return both[:, 4 * core : 4 * core + 4, :].astype(BF)

        send_a[0] = rows(far, 1 - low)
        send_a[1] = rows(across, 1 - low)
        send_b[0] = rows(y, 1 - low)
        send_b[1] = rows(near, 1 - low)
        keep_a[0] = rows(near, low)
        keep_a[1] = rows(across, low)
        keep_b[0] = rows(y, low)
        keep_b[1] = rows(far, low)

    pl.when(c == 0)(lambda: emit(0))
    pl.when(c == 1)(lambda: emit(1))


def split_rows(grads, mb):
    _, m, rows, cols = grads.shape
    two = pl.BlockSpec((2, mb, 4, cols), lambda i: (0, i, 0, 0))
    return pl.pallas_call(
        split_kernel,
        grid=(m // mb,),
        in_specs=[pl.BlockSpec((1, mb, rows, cols), lambda i: (0, i, 0, 0))],
        out_specs=[two] * 4,
        out_shape=[sds((2, m, 4, cols), BF)] * 4,
        scratch_shapes=[pltpu.VMEM((mb, rows, cols), F32)],
        compiler_params=params(48),
        name="split_rows",
    )(grads)


def momentum_kernel(slots, keep, swapped, first, second, mom, nesterov, new_mom):
    m = mom.shape[0]

    def step(j, carry):
        mat = slots[j]
        gradient = (keep[0, j].astype(F32) + swapped[0, j].astype(F32)) + (
            first[0, j].astype(F32) + second[j].astype(F32)
        )
        new = DECAY * mom[mat] + gradient
        new_mom[mat] = new
        nesterov[mat] = (gradient + DECAY * new).astype(BF)
        return carry

    lax.fori_loop(0, m, step, 0, unroll=min(8, m))


def momentum_step(slots, keep, swapped, first, second, mom):
    m, _, cols = mom.shape
    return pl.pallas_call(
        momentum_kernel,
        in_specs=[pl.BlockSpec(memory_space=SMEM)] + whole(5),
        out_specs=whole(2),
        out_shape=[sds((m, 4, cols), BF), sds((m, 4, cols), F32)],
        compiler_params=params(),
        name="momentum_step",
    )(slots, keep, swapped, first, second, mom)


def blocks_of(cols):
    n = cols // 128
    return [(i, j) for i in range(n) for j in range(i, n)]


def gram_kernel(a_ref, rows_ref, gram):
    count, _, cols = a_ref.shape
    for g in range(count // 4):
        four = [a_ref[4 * g + i].astype(F32) for i in range(4)]
        rows_ref[16 * g : 16 * g + 16, :] = jnp.concatenate(four, axis=0).astype(BF)
    n = cols // 128
    b = 0
    for i in range(n):
        strip = lax.dot_general(
            rows_ref[:, 128 * i : 128 * i + 128],
            rows_ref[:, 128 * i :],
            (((0,), (0,)), ((), ())),
            preferred_element_type=F32,
        )
        for j in range(i, n):
            gram[128 * b : 128 * b + 128, :] = strip[:, 128 * (j - i) : 128 * (j - i) + 128].astype(BF)
            b += 1


def partial_gram(a):
    count, _, cols = a.shape
    nb = len(blocks_of(cols))
    return pl.pallas_call(
        gram_kernel,
        in_specs=whole(1),
        out_specs=whole(2),
        out_shape=[sds((4 * count, cols), BF), sds((nb * 128, 128), BF)],
        compiler_params=params(),
        name="partial_gram",
    )(a)


def polish_kernel(scale, gram, rows_ref, out, level, low, poly, high):
    count, cols = rows_ref.shape
    n = cols // 128

    def block_of(b):
        return gram[128 * b : 128 * b + 128, :].astype(F32)

    eye = (
        lax.broadcasted_iota(jnp.int32, (128, 128), 0) == lax.broadcasted_iota(jnp.int32, (128, 128), 1)
    )
    diag = jnp.zeros((128, 128), F32)
    for b, (i, j) in enumerate(blocks_of(cols)):
        if i == j:
            diag += block_of(b)
    trace = jnp.sum(jnp.where(eye, diag, 0.0))
    inv_norm = 1.0 / (jnp.sqrt(jnp.full((1, 1), trace)) + 1e-7)
    square = inv_norm * inv_norm
    for b, (i, j) in enumerate(blocks_of(cols)):
        block = block_of(b) * square
        level[128 * i : 128 * i + 128, 128 * j : 128 * j + 128] = block
        low[128 * i : 128 * i + 128, 128 * j : 128 * j + 128] = block.astype(BF)
        if i != j:
            block = block.T
            level[128 * j : 128 * j + 128, 128 * i : 128 * i + 128] = block
            low[128 * j : 128 * j + 128, 128 * i : 128 * i + 128] = block.astype(BF)

    step = 256 if cols % 256 == 0 else 128
    for r in range(0, cols, step):
        part = jnp.dot(low[r : r + step, :], low[...], preferred_element_type=F32)
        poly[r : r + step, :] = (COEF_B * level[r : r + step, :] + COEF_C * part).astype(BF)
    for r in range(0, cols, step):
        part = jnp.dot(poly[r : r + step, :], low[...], preferred_element_type=F32)
        left_now = COEF_A * level[r : r + step, :] + part
        left_low = left_now.astype(BF)
        high[r : r + step, :] = (
            COEF_A * left_now + jnp.dot(left_low, poly[...], preferred_element_type=F32)
        ).astype(BF)
    rows = rows_ref[...]
    y0 = COEF_A * rows.astype(F32) + jnp.dot(rows, poly[...], preferred_element_type=F32)
    y1 = jnp.dot(y0.astype(BF), high[...], preferred_element_type=F32)
    y2 = jnp.dot(y1.astype(BF), high[...], preferred_element_type=F32)
    result = (COEF_A * y0 + COEF_B * y1 + COEF_C * y2) * (scale * inv_norm)
    for i in range(count // 4):
        out[i] = result[4 * i : 4 * i + 4, :].astype(BF)


def polish(scale, gram, rows):
    count, cols = rows.shape
    return pl.pallas_call(
        functools.partial(polish_kernel, scale),
        in_specs=whole(2),
        out_specs=whole(1)[0],
        out_shape=sds((count // 4, 4, cols), BF),
        scratch_shapes=[
            pltpu.VMEM((cols, cols), F32),
            pltpu.VMEM((cols, cols), BF),
            pltpu.VMEM((cols, cols), BF),
            pltpu.VMEM((cols, cols), BF),
        ],
        compiler_params=params(32),
        name="polish",
    )(gram, rows)


def core_swap(v):
    return lax.ppermute(v, "dp", [(i, i ^ 1) for i in range(2 * NY)])


def y_swap(v, second):
    perm = []
    for y in range(NY):
        for c in range(2):
            to = (y ^ 1) if c == second else NY - 1 - y
            perm.append((2 * y + c, 2 * to + c))
    return lax.ppermute(v, "dp", perm)


def shards(n_rows, grads, momentum, slot_matrix):
    m = grads.shape[1]
    cols = grads.shape[3]

    send_a, send_b, keep_a, keep_b = split_rows(grads, min(8, m))
    swapped_a = core_swap(send_a)
    swapped_b = core_swap(send_b)
    first = y_swap((keep_a.astype(F32) + swapped_a.astype(F32)).astype(BF), 0)
    far = (keep_b[1].astype(F32) + swapped_b[1].astype(F32)) + first[1].astype(F32)
    second = y_swap(far.astype(BF), 1)
    nesterov, new_momentum = momentum_step(slot_matrix, keep_b, swapped_b, first, second, momentum)

    mine = lax.all_to_all(nesterov, "fsdp", split_axis=0, concat_axis=0, tiled=True)

    rows, gram = partial_gram(mine)
    gram = lax.psum(gram, "dp")

    update = polish(math.sqrt(max(n_rows, cols)), gram, rows)
    update = lax.all_to_all(update, "fsdp", split_axis=0, concat_axis=0, tiled=True)
    return (update, new_momentum)


def solution(mesh):
    in_specs = (P("dp", None, "fsdp", None), P(None, ("fsdp", "dp"), None), P())
    out_specs = (P(None, ("fsdp", "dp"), None), P(None, ("fsdp", "dp"), None))

    def run(grads, momentum, slot_matrix):
        body = functools.partial(shards, grads.shape[2])
        return jax.shard_map(body, mesh=mesh, in_specs=in_specs, out_specs=out_specs, check_vma=False)(
            grads, momentum, slot_matrix
        )

    return run
```

```python
import functools
import math

import jax
import jax.numpy as jnp
import numpy as np
from jax import lax
from jax.experimental import pallas as pl
from jax.experimental.pallas import tpu as pltpu
from jax.sharding import PartitionSpec as P

NY = 4
COEF_A = 3.4445
COEF_B = -4.775
COEF_C = 2.0315
DECAY = 0.95
BF = jnp.bfloat16
F32 = jnp.float32
SMEM = pltpu.SMEM


def sds(shape, dtype):
    return jax.ShapeDtypeStruct(shape, dtype)


def params(mib=16):
    return pltpu.CompilerParams(vmem_limit_bytes=mib * 1024 * 1024)


def whole(n):
    return [pl.BlockSpec(memory_space=pltpu.VMEM)] * n


def place_of():
    d = lax.axis_index("dp")
    y, c = lax.div(d, 2), lax.rem(d, 2)
    flip, turn = y + 1 - 2 * lax.rem(y, 2), NY - 1 - y
    near = jnp.where(c == 0, flip, turn)
    far = jnp.where(c == 0, turn, flip)
    return y, c, near, far, lax.rem(y + 2, NY)


def split_kernel(g_hbm, send_across, send_rest, keep_across, keep_rest, raw, wide, sems):
    y, c, near, far, across = place_of()
    parts = sems.shape[0]
    mb = raw.shape[0] // parts

    def fetch(i):
        return pltpu.make_async_copy(
            g_hbm.at[0, pl.ds(i * mb, mb)], raw.at[pl.ds(i * mb, mb)], sems.at[i]
        )

    for i in range(parts):
        fetch(i).start()

    def emit(i, low):
        here = pl.ds(i * mb, mb)

        def rows(yy, core):
            both = wide[:, pl.ds(pl.multiple_of(8 * yy, 8), 8), :]
            return both[:, 4 * core : 4 * core + 4, :].astype(BF)

        send_across[here] = rows(across, 1 - low)
        send_rest[0, here] = rows(y, 1 - low)
        send_rest[1, here] = rows(near, 1 - low)
        send_rest[2, here] = rows(far, 1 - low)
        keep_across[here] = rows(across, low)
        keep_rest[0, here] = rows(y, low)
        keep_rest[1, here] = rows(far, low)
        keep_rest[2, here] = rows(near, low)

    for i in range(parts):
        fetch(i).wait()
        wide[...] = raw[i * mb : i * mb + mb].astype(F32)
        pl.when(c == 0)(functools.partial(emit, i, 0))
        pl.when(c == 1)(functools.partial(emit, i, 1))


def split_rows(grads, parts):
    _, m, rows, cols = grads.shape
    one, three = sds((m, 4, cols), BF), sds((3, m, 4, cols), BF)
    return pl.pallas_call(
        split_kernel,
        in_specs=[pl.BlockSpec(memory_space=pl.ANY)],
        out_specs=whole(4),
        out_shape=[one, three, one, three],
        scratch_shapes=[
            pltpu.VMEM((m, rows, cols), BF),
            pltpu.VMEM((m // parts, rows, cols), F32),
            pltpu.SemaphoreType.DMA((parts,)),
        ],
        compiler_params=params(48),
        name="split_rows",
    )(grads)


def momentum_kernel(slots, keep, swapped, first, second, mom, nesterov, new_mom):
    m = mom.shape[0]

    def step(j, carry):
        mat = slots[j]
        gradient = (keep[0, j].astype(F32) + swapped[0, j].astype(F32)) + (
            first[j].astype(F32) + second[j].astype(F32)
        )
        new = DECAY * mom[mat] + gradient
        new_mom[mat] = new
        nesterov[mat] = (gradient + DECAY * new).astype(BF)
        return carry

    lax.fori_loop(0, m, step, 0, unroll=min(8, m))


def momentum_step(slots, keep, swapped, first, second, mom):
    m, _, cols = mom.shape
    return pl.pallas_call(
        momentum_kernel,
        in_specs=[pl.BlockSpec(memory_space=SMEM)] + whole(5),
        out_specs=whole(2),
        out_shape=[sds((m, 4, cols), BF), sds((m, 4, cols), F32)],
        compiler_params=params(),
        name="momentum_step",
    )(slots, keep, swapped, first, second, mom)


def blocks_of(cols):
    n = cols // 128
    return [(i, j) for i in range(n) for j in range(i, n)]


def gram_kernel(a_ref, rows_ref, send, keep, slabs):
    c = lax.rem(lax.axis_index("dp"), 2)
    count, _, cols = a_ref.shape
    for g in range(count // 4):
        four = [a_ref[4 * g + i].astype(F32) for i in range(4)]
        rows_ref[16 * g : 16 * g + 16, :] = jnp.concatenate(four, axis=0).astype(BF)
    n = cols // 128
    b = 0
    for i in range(n):
        strip = lax.dot_general(
            rows_ref[:, 128 * i : 128 * i + 128],
            rows_ref[:, 128 * i :],
            (((0,), (0,)), ((), ())),
            preferred_element_type=F32,
        )
        for j in range(i, n):
            block = strip[:, 128 * (j - i) : 128 * (j - i) + 128]
            slabs[0, b] = block[:64, :]
            slabs[1, b] = block[64:, :]
            b += 1
    send[...] = slabs[1 - c].astype(BF)
    keep[...] = slabs[c]


def partial_gram(a):
    count, _, cols = a.shape
    nb = len(blocks_of(cols))
    return pl.pallas_call(
        gram_kernel,
        in_specs=whole(1),
        out_specs=whole(3),
        out_shape=[
            sds((4 * count, cols), BF),
            sds((nb, 64, 128), BF),
            sds((nb, 64, 128), F32),
        ],
        scratch_shapes=[pltpu.VMEM((2, nb, 64, 128), F32)],
        compiler_params=params(),
        name="partial_gram",
    )(a)


def polish_kernel(scale, own, other, rows_ref, out, slabs, level, low, poly, high):
    c = lax.rem(lax.axis_index("dp"), 2)
    count, cols = rows_ref.shape
    n = cols // 128
    slabs[c] = own[...].astype(F32)
    slabs[1 - c] = other[...].astype(F32)

    eye = (
        lax.broadcasted_iota(jnp.int32, (128, 128), 0) == lax.broadcasted_iota(jnp.int32, (128, 128), 1)
    )
    diag = jnp.zeros((128, 128), F32)
    for b, (i, j) in enumerate(blocks_of(cols)):
        if i == j:
            diag += slabs[:, b].reshape(128, 128)
    trace = jnp.sum(jnp.where(eye, diag, 0.0))
    inv_norm = 1.0 / (jnp.sqrt(jnp.full((1, 1), trace)) + 1e-7)
    square = inv_norm * inv_norm
    for b, (i, j) in enumerate(blocks_of(cols)):
        block = slabs[:, b].reshape(128, 128) * square
        level[128 * i : 128 * i + 128, 128 * j : 128 * j + 128] = block
        low[128 * i : 128 * i + 128, 128 * j : 128 * j + 128] = block.astype(BF)
        if i != j:
            block = block.T
            level[128 * j : 128 * j + 128, 128 * i : 128 * i + 128] = block
            low[128 * j : 128 * j + 128, 128 * i : 128 * i + 128] = block.astype(BF)

    step = 256 if cols % 256 == 0 else 128
    for r in range(0, cols, step):
        part = jnp.dot(low[r : r + step, :], low[...], preferred_element_type=F32)
        poly[r : r + step, :] = (COEF_B * level[r : r + step, :] + COEF_C * part).astype(BF)
    for r in range(0, cols, step):
        part = jnp.dot(poly[r : r + step, :], low[...], preferred_element_type=F32)
        left_now = COEF_A * level[r : r + step, :] + part
        left_low = left_now.astype(BF)
        high[r : r + step, :] = (
            COEF_A * left_now + jnp.dot(left_low, poly[...], preferred_element_type=F32)
        ).astype(BF)
    rows = rows_ref[...]
    y0 = COEF_A * rows.astype(F32) + jnp.dot(rows, poly[...], preferred_element_type=F32)
    y1 = jnp.dot(y0.astype(BF), high[...], preferred_element_type=F32)
    y2 = jnp.dot(y1.astype(BF), high[...], preferred_element_type=F32)
    result = (COEF_A * y0 + COEF_B * y1 + COEF_C * y2) * (scale * inv_norm)
    for i in range(count // 4):
        out[i] = result[4 * i : 4 * i + 4, :].astype(BF)


def polish(scale, own, other, rows):
    count, cols = rows.shape
    nb = own.shape[0]
    return pl.pallas_call(
        functools.partial(polish_kernel, scale),
        in_specs=whole(3),
        out_specs=whole(1)[0],
        out_shape=sds((count // 4, 4, cols), BF),
        scratch_shapes=[
            pltpu.VMEM((2, nb, 64, 128), F32),
            pltpu.VMEM((cols, cols), F32),
            pltpu.VMEM((cols, cols), BF),
            pltpu.VMEM((cols, cols), BF),
            pltpu.VMEM((cols, cols), BF),
        ],
        compiler_params=params(32),
        name="polish",
    )(own, other, rows)


def core_swap(v):
    return lax.ppermute(v, "dp", [(i, i ^ 1) for i in range(2 * NY)])


def y_swap(v, second):
    perm = []
    for y in range(NY):
        for c in range(2):
            to = (y ^ 1) if c == second else NY - 1 - y
            perm.append((2 * y + c, 2 * to + c))
    return lax.ppermute(v, "dp", perm)


def exchange(v):
    order = np.random.RandomState(7).permutation(v.shape[0])
    groups = [[int(i) for i in order]]
    return lax.all_to_all(v, "fsdp", split_axis=0, concat_axis=0, axis_index_groups=groups, tiled=True)


def shards(n_rows, grads, momentum, slot_matrix):
    m = grads.shape[1]
    cols = grads.shape[3]

    send_across, send_rest, keep_across, keep_rest = split_rows(grads, 8)
    across = keep_across.astype(F32) + core_swap(send_across).astype(F32)
    first_far = y_swap(across.astype(BF), 0)
    swapped = core_swap(send_rest)
    first_own = y_swap((keep_rest[2].astype(F32) + swapped[2].astype(F32)).astype(BF), 0)
    far = (keep_rest[1].astype(F32) + swapped[1].astype(F32)) + first_far.astype(F32)
    second = y_swap(far.astype(BF), 1)
    nesterov, new_momentum = momentum_step(slot_matrix, keep_rest, swapped, first_own, second, momentum)

    mine = exchange(nesterov)

    rows, gram_send, gram_keep = partial_gram(mine)
    gram = gram_keep + core_swap(gram_send).astype(F32)
    gram = gram + y_swap(gram.astype(BF), 0).astype(F32)
    gram = gram + y_swap(gram.astype(BF), 1).astype(F32)
    own = gram.astype(BF)
    other = core_swap(own)

    update = polish(math.sqrt(max(n_rows, cols)), own, other, rows)
    return (exchange(update), new_momentum)


def solution(mesh):
    in_specs = (P("dp", None, "fsdp", None), P(None, ("fsdp", "dp"), None), P())
    out_specs = (P(None, ("fsdp", "dp"), None), P(None, ("fsdp", "dp"), None))

    def run(grads, momentum, slot_matrix):
        body = functools.partial(shards, grads.shape[2])
        return jax.shard_map(body, mesh=mesh, in_specs=in_specs, out_specs=out_specs, check_vma=False)(
            grads, momentum, slot_matrix
        )

    return run
```

```python
import functools
import math

import jax
import jax.numpy as jnp
from jax import lax
from jax.experimental import pallas as pl
from jax.experimental.pallas import tpu as pltpu
from jax.sharding import PartitionSpec as P

NY = 4
COEF_A = 3.4445
COEF_B = -4.775
COEF_C = 2.0315
DECAY = 0.95
BF = jnp.bfloat16
F32 = jnp.float32
SMEM = pltpu.SMEM


def sds(shape, dtype):
    return jax.ShapeDtypeStruct(shape, dtype)


def params(mib=16):
    return pltpu.CompilerParams(vmem_limit_bytes=mib * 1024 * 1024)


def whole(n):
    return [pl.BlockSpec(memory_space=pltpu.VMEM)] * n


def place_of():
    d = lax.axis_index("dp")
    y, c = lax.div(d, 2), lax.rem(d, 2)
    flip, turn = y + 1 - 2 * lax.rem(y, 2), NY - 1 - y
    near = jnp.where(c == 0, flip, turn)
    far = jnp.where(c == 0, turn, flip)
    return y, c, near, far, lax.rem(y + 2, NY)


def split_kernel(g_hbm, send_across, send_rest, keep_across, keep_rest, raw, wide, sems):
    y, c, near, far, across = place_of()
    parts = sems.shape[0]
    mb = raw.shape[0] // parts

    def fetch(i):
        return pltpu.make_async_copy(
            g_hbm.at[0, pl.ds(i * mb, mb)], raw.at[pl.ds(i * mb, mb)], sems.at[i]
        )

    for i in range(parts):
        fetch(i).start()

    def emit(i, low):
        here = pl.ds(i * mb, mb)

        def rows(yy, core):
            both = wide[:, pl.ds(pl.multiple_of(8 * yy, 8), 8), :]
            return both[:, 4 * core : 4 * core + 4, :].astype(BF)

        send_across[here] = rows(across, 1 - low)
        send_rest[0, here] = rows(y, 1 - low)
        send_rest[1, here] = rows(near, 1 - low)
        send_rest[2, here] = rows(far, 1 - low)
        keep_across[here] = rows(across, low)
        keep_rest[0, here] = rows(y, low)
        keep_rest[1, here] = rows(far, low)
        keep_rest[2, here] = rows(near, low)

    for i in range(parts):
        fetch(i).wait()
        wide[...] = raw[i * mb : i * mb + mb].astype(F32)
        pl.when(c == 0)(functools.partial(emit, i, 0))
        pl.when(c == 1)(functools.partial(emit, i, 1))


def split_rows(grads, parts):
    _, m, rows, cols = grads.shape
    one, three = sds((m, 4, cols), BF), sds((3, m, 4, cols), BF)
    return pl.pallas_call(
        split_kernel,
        in_specs=[pl.BlockSpec(memory_space=pl.ANY)],
        out_specs=whole(4),
        out_shape=[one, three, one, three],
        scratch_shapes=[
            pltpu.VMEM((m, rows, cols), BF),
            pltpu.VMEM((m // parts, rows, cols), F32),
            pltpu.SemaphoreType.DMA((parts,)),
        ],
        compiler_params=params(48),
        name="split_rows",
    )(grads)


def momentum_kernel(slots, keep, swapped, first, second, mom, nesterov, new_mom):
    m, _, cols = mom.shape
    half = cols // 2

    def step(j, carry):
        mat = slots[j]
        gradient = (keep[0, j].astype(F32) + swapped[0, j].astype(F32)) + (
            first[j].astype(F32) + second[j].astype(F32)
        )
        new = DECAY * mom[mat] + gradient
        new_mom[mat] = new
        value = gradient + DECAY * new
        nesterov[mat] = jnp.concatenate([value[:, :half], value[:, half:]], axis=0).astype(BF)
        return carry

    lax.fori_loop(0, m, step, 0, unroll=min(8, m))


def momentum_step(slots, keep, swapped, first, second, mom):
    m, _, cols = mom.shape
    return pl.pallas_call(
        momentum_kernel,
        in_specs=[pl.BlockSpec(memory_space=SMEM)] + whole(5),
        out_specs=whole(2),
        out_shape=[sds((m, 8, cols // 2), BF), sds((m, 4, cols), F32)],
        compiler_params=params(),
        name="momentum_step",
    )(slots, keep, swapped, first, second, mom)


def blocks_of(cols):
    n = cols // 128
    return [(i, j) for i in range(n) for j in range(i, n)]


def gram_kernel(a_ref, rows_ref, gram):
    count, _, half = a_ref.shape
    for g in range(count // 4):
        four = [a_ref[4 * g + i].astype(F32) for i in range(4)]
        here = slice(16 * g, 16 * g + 16)
        rows_ref[here, :half] = jnp.concatenate([v[:4] for v in four], axis=0).astype(BF)
        rows_ref[here, half:] = jnp.concatenate([v[4:] for v in four], axis=0).astype(BF)
    n = 2 * half // 128
    b = 0
    for i in range(n):
        strip = lax.dot_general(
            rows_ref[:, 128 * i : 128 * i + 128],
            rows_ref[:, 128 * i :],
            (((0,), (0,)), ((), ())),
            preferred_element_type=F32,
        )
        for j in range(i, n):
            block = strip[:, 128 * (j - i) : 128 * (j - i) + 128].astype(BF)
            for k in range(8):
                gram[k, 16 * b : 16 * b + 16, :] = block[16 * k : 16 * k + 16, :]
            b += 1


def partial_gram(a):
    count, _, half = a.shape
    nb = len(blocks_of(2 * half))
    return pl.pallas_call(
        gram_kernel,
        in_specs=whole(1),
        out_specs=whole(2),
        out_shape=[sds((4 * count, 2 * half), BF), sds((8, 16 * nb, 128), BF)],
        compiler_params=params(),
        name="partial_gram",
    )(a)


def polish_kernel(scale, gram, rows_ref, out, level, low, poly, high):
    count, cols = rows_ref.shape
    n = cols // 128

    def block_of(b):
        return gram[:, 16 * b : 16 * b + 16, :].reshape(128, 128).astype(F32)

    eye = (
        lax.broadcasted_iota(jnp.int32, (128, 128), 0) == lax.broadcasted_iota(jnp.int32, (128, 128), 1)
    )
    diag = jnp.zeros((128, 128), F32)
    for b, (i, j) in enumerate(blocks_of(cols)):
        if i == j:
            diag += block_of(b)
    trace = jnp.sum(jnp.where(eye, diag, 0.0))
    inv_norm = 1.0 / (jnp.sqrt(jnp.full((1, 1), trace)) + 1e-7)
    square = inv_norm * inv_norm
    for b, (i, j) in enumerate(blocks_of(cols)):
        block = block_of(b) * square
        level[128 * i : 128 * i + 128, 128 * j : 128 * j + 128] = block
        low[128 * i : 128 * i + 128, 128 * j : 128 * j + 128] = block.astype(BF)
        if i != j:
            block = block.T
            level[128 * j : 128 * j + 128, 128 * i : 128 * i + 128] = block
            low[128 * j : 128 * j + 128, 128 * i : 128 * i + 128] = block.astype(BF)

    step = 256 if cols % 256 == 0 else 128
    for r in range(0, cols, step):
        part = jnp.dot(low[r : r + step, :], low[...], preferred_element_type=F32)
        poly[r : r + step, :] = (COEF_B * level[r : r + step, :] + COEF_C * part).astype(BF)
    for r in range(0, cols, step):
        part = jnp.dot(poly[r : r + step, :], low[...], preferred_element_type=F32)
        left_now = COEF_A * level[r : r + step, :] + part
        left_low = left_now.astype(BF)
        high[r : r + step, :] = (
            COEF_A * left_now + jnp.dot(left_low, poly[...], preferred_element_type=F32)
        ).astype(BF)
    rows = rows_ref[...]
    y0 = COEF_A * rows.astype(F32) + jnp.dot(rows, poly[...], preferred_element_type=F32)
    y1 = jnp.dot(y0.astype(BF), high[...], preferred_element_type=F32)
    y2 = jnp.dot(y1.astype(BF), high[...], preferred_element_type=F32)
    result = (COEF_A * y0 + COEF_B * y1 + COEF_C * y2) * (scale * inv_norm)
    for i in range(count // 4):
        out[i] = result[4 * i : 4 * i + 4, :].astype(BF)


def polish(scale, gram, rows):
    count, cols = rows.shape
    return pl.pallas_call(
        functools.partial(polish_kernel, scale),
        in_specs=whole(2),
        out_specs=whole(1)[0],
        out_shape=sds((count // 4, 4, cols), BF),
        scratch_shapes=[
            pltpu.VMEM((cols, cols), F32),
            pltpu.VMEM((cols, cols), BF),
            pltpu.VMEM((cols, cols), BF),
            pltpu.VMEM((cols, cols), BF),
        ],
        compiler_params=params(32),
        name="polish",
    )(gram, rows)


def core_swap(v):
    return lax.ppermute(v, "dp", [(i, i ^ 1) for i in range(2 * NY)])


def y_swap(v, second):
    perm = []
    for y in range(NY):
        for c in range(2):
            to = (y ^ 1) if c == second else NY - 1 - y
            perm.append((2 * y + c, 2 * to + c))
    return lax.ppermute(v, "dp", perm)


def exchange(v, axis):
    return lax.all_to_all(v, axis, split_axis=0, concat_axis=0, tiled=True)


def shards(n_rows, grads, momentum, slot_matrix):
    m = grads.shape[1]
    cols = grads.shape[3]

    send_across, send_rest, keep_across, keep_rest = split_rows(grads, 8)
    across = (keep_across.astype(F32) + core_swap(send_across).astype(F32)).astype(BF)
    across, send_rest = lax.optimization_barrier((across, send_rest))
    first_far = y_swap(across, 0)
    swapped = core_swap(send_rest)
    first_own = y_swap((keep_rest[2].astype(F32) + swapped[2].astype(F32)).astype(BF), 0)
    far = (keep_rest[1].astype(F32) + swapped[1].astype(F32)) + first_far.astype(F32)
    second = y_swap(far.astype(BF), 1)
    nesterov, new_momentum = momentum_step(slot_matrix, keep_rest, swapped, first_own, second, momentum)

    mine = exchange(nesterov, "fsdp")

    rows, gram = partial_gram(mine)
    summed = jnp.sum(exchange(gram, "dp").astype(F32), axis=0).astype(BF)
    gram = exchange(jnp.broadcast_to(summed[None], gram.shape), "dp")

    update = polish(math.sqrt(max(n_rows, cols)), gram, rows)
    return (exchange(update, "fsdp"), new_momentum)


def solution(mesh):
    in_specs = (P("dp", None, "fsdp", None), P(None, ("fsdp", "dp"), None), P())
    out_specs = (P(None, ("fsdp", "dp"), None), P(None, ("fsdp", "dp"), None))

    def run(grads, momentum, slot_matrix):
        body = functools.partial(shards, grads.shape[2])
        return jax.shard_map(body, mesh=mesh, in_specs=in_specs, out_specs=out_specs, check_vma=False)(
            grads, momentum, slot_matrix
        )

    return run
```

```python
import functools
import math

import jax
import jax.numpy as jnp
from jax import lax
from jax.experimental import pallas as pl
from jax.experimental.pallas import tpu as pltpu
from jax.sharding import PartitionSpec as P

NY = 4
COEF_A = 3.4445
COEF_B = -4.775
COEF_C = 2.0315
DECAY = 0.95
BF = jnp.bfloat16
F32 = jnp.float32
SMEM = pltpu.SMEM


def sds(shape, dtype):
    return jax.ShapeDtypeStruct(shape, dtype)


def params(mib=16):
    return pltpu.CompilerParams(vmem_limit_bytes=mib * 1024 * 1024)


def whole(n):
    return [pl.BlockSpec(memory_space=pltpu.VMEM)] * n


def place_of():
    d = lax.axis_index("dp")
    y, c = lax.div(d, 2), lax.rem(d, 2)
    flip, turn = y + 1 - 2 * lax.rem(y, 2), NY - 1 - y
    near = jnp.where(c == 0, flip, turn)
    far = jnp.where(c == 0, turn, flip)
    return y, c, near, far, lax.rem(y + 2, NY)


def split_kernel(g_hbm, send_a, send_b, keep_a, keep_b, raw, wide, sems):
    y, c, near, far, across = place_of()
    parts = sems.shape[0]
    mb = raw.shape[0] // parts

    def fetch(i):
        return pltpu.make_async_copy(
            g_hbm.at[0, pl.ds(i * mb, mb)], raw.at[pl.ds(i * mb, mb)], sems.at[i]
        )

    for i in range(parts):
        fetch(i).start()

    def emit(i, low):
        here = pl.ds(i * mb, mb)

        def rows(yy, core):
            both = wide[:, pl.ds(pl.multiple_of(8 * yy, 8), 8), :]
            return both[:, 4 * core : 4 * core + 4, :].astype(BF)

        send_a[0, here] = rows(across, 1 - low)
        send_a[1, here] = rows(far, 1 - low)
        send_b[0, here] = rows(y, 1 - low)
        send_b[1, here] = rows(near, 1 - low)
        keep_a[0, here] = rows(across, low)
        keep_a[1, here] = rows(near, low)
        keep_b[0, here] = rows(y, low)
        keep_b[1, here] = rows(far, low)

    for i in range(parts):
        fetch(i).wait()
        wide[...] = raw[i * mb : i * mb + mb].astype(F32)
        pl.when(c == 0)(functools.partial(emit, i, 0))
        pl.when(c == 1)(functools.partial(emit, i, 1))


def split_rows(grads, parts):
    _, m, rows, cols = grads.shape
    two = sds((2, m, 4, cols), BF)
    return pl.pallas_call(
        split_kernel,
        in_specs=[pl.BlockSpec(memory_space=pl.ANY)],
        out_specs=whole(4),
        out_shape=[two] * 4,
        scratch_shapes=[
            pltpu.VMEM((m, rows, cols), BF),
            pltpu.VMEM((m // parts, rows, cols), F32),
            pltpu.SemaphoreType.DMA((parts,)),
        ],
        compiler_params=params(48),
        name="split_rows",
    )(grads)


def gradient_at(j, keep, swapped, first, second):
    return (keep[0, j].astype(F32) + swapped[0, j].astype(F32)) + (
        first[j].astype(F32) + second[j].astype(F32)
    )


def nesterov_kernel(slots, keep, swapped, first, second, mom, nesterov):
    def step(j, carry):
        mat = slots[j]
        gradient = gradient_at(j, keep, swapped, first, second)
        nesterov[mat] = (gradient + DECAY * (DECAY * mom[mat] + gradient)).astype(BF)
        return carry

    m = mom.shape[0]
    lax.fori_loop(0, m, step, 0, unroll=min(8, m))


def momentum_kernel(slots, keep, swapped, first, second, mom, new_mom):
    def step(j, carry):
        mat = slots[j]
        new_mom[mat] = DECAY * mom[mat] + gradient_at(j, keep, swapped, first, second)
        return carry

    m = mom.shape[0]
    lax.fori_loop(0, m, step, 0, unroll=min(8, m))


def momentum_call(kernel, dtype, name, *args):
    mom = args[-1]
    return pl.pallas_call(
        kernel,
        in_specs=[pl.BlockSpec(memory_space=SMEM)] + whole(5),
        out_specs=whole(1)[0],
        out_shape=sds(mom.shape, dtype),
        compiler_params=params(),
        cost_estimate=pl.CostEstimate(flops=6 * mom.size, bytes_accessed=16 * mom.size, transcendentals=0),
        name=name,
    )(*args)


def blocks_of(cols):
    n = cols // 128
    return [(i, j) for i in range(n) for j in range(i, n)]


def gram_kernel(a_ref, rows_ref, send, keep, slabs):
    c = lax.rem(lax.axis_index("dp"), 2)
    count, _, cols = a_ref.shape
    for g in range(count // 4):
        four = [a_ref[4 * g + i].astype(F32) for i in range(4)]
        rows_ref[16 * g : 16 * g + 16, :] = jnp.concatenate(four, axis=0).astype(BF)
    n = cols // 128
    b = 0
    for i in range(n):
        strip = lax.dot_general(
            rows_ref[:, 128 * i : 128 * i + 128],
            rows_ref[:, 128 * i :],
            (((0,), (0,)), ((), ())),
            preferred_element_type=F32,
        )
        for j in range(i, n):
            block = strip[:, 128 * (j - i) : 128 * (j - i) + 128]
            slabs[0, b] = block[:64, :]
            slabs[1, b] = block[64:, :]
            b += 1
    send[...] = slabs[1 - c].astype(BF)
    keep[...] = slabs[c]


def partial_gram(a):
    count, _, cols = a.shape
    nb = len(blocks_of(cols))
    return pl.pallas_call(
        gram_kernel,
        in_specs=whole(1),
        out_specs=whole(3),
        out_shape=[
            sds((4 * count, cols), BF),
            sds((nb, 64, 128), BF),
            sds((nb, 64, 128), F32),
        ],
        scratch_shapes=[pltpu.VMEM((2, nb, 64, 128), F32)],
        compiler_params=params(),
        name="partial_gram",
    )(a)


def polish_kernel(scale, own, other, rows_ref, out, slabs, level, low, poly, high):
    c = lax.rem(lax.axis_index("dp"), 2)
    count, cols = rows_ref.shape
    n = cols // 128
    slabs[c] = own[...].astype(F32)
    slabs[1 - c] = other[...].astype(F32)

    eye = (
        lax.broadcasted_iota(jnp.int32, (128, 128), 0) == lax.broadcasted_iota(jnp.int32, (128, 128), 1)
    )
    diag = jnp.zeros((128, 128), F32)
    for b, (i, j) in enumerate(blocks_of(cols)):
        if i == j:
            diag += slabs[:, b].reshape(128, 128)
    trace = jnp.sum(jnp.where(eye, diag, 0.0))
    inv_norm = 1.0 / (jnp.sqrt(jnp.full((1, 1), trace)) + 1e-7)
    square = inv_norm * inv_norm
    for b, (i, j) in enumerate(blocks_of(cols)):
        block = slabs[:, b].reshape(128, 128) * square
        level[128 * i : 128 * i + 128, 128 * j : 128 * j + 128] = block
        low[128 * i : 128 * i + 128, 128 * j : 128 * j + 128] = block.astype(BF)
        if i != j:
            block = block.T
            level[128 * j : 128 * j + 128, 128 * i : 128 * i + 128] = block
            low[128 * j : 128 * j + 128, 128 * i : 128 * i + 128] = block.astype(BF)

    step = 256 if cols % 256 == 0 else 128
    for r in range(0, cols, step):
        part = jnp.dot(low[r : r + step, :], low[...], preferred_element_type=F32)
        poly[r : r + step, :] = (COEF_B * level[r : r + step, :] + COEF_C * part).astype(BF)
    for r in range(0, cols, step):
        part = jnp.dot(poly[r : r + step, :], low[...], preferred_element_type=F32)
        left_now = COEF_A * level[r : r + step, :] + part
        left_low = left_now.astype(BF)
        high[r : r + step, :] = (
            COEF_A * left_now + jnp.dot(left_low, poly[...], preferred_element_type=F32)
        ).astype(BF)
    rows = rows_ref[...]
    y0 = COEF_A * rows.astype(F32) + jnp.dot(rows, poly[...], preferred_element_type=F32)
    y1 = jnp.dot(y0.astype(BF), high[...], preferred_element_type=F32)
    y2 = jnp.dot(y1.astype(BF), high[...], preferred_element_type=F32)
    result = (COEF_A * y0 + COEF_B * y1 + COEF_C * y2) * (scale * inv_norm)
    for i in range(count // 4):
        out[i] = result[4 * i : 4 * i + 4, :].astype(BF)


def polish(scale, own, other, rows):
    count, cols = rows.shape
    nb = own.shape[0]
    return pl.pallas_call(
        functools.partial(polish_kernel, scale),
        in_specs=whole(3),
        out_specs=whole(1)[0],
        out_shape=sds((count // 4, 4, cols), BF),
        scratch_shapes=[
            pltpu.VMEM((2, nb, 64, 128), F32),
            pltpu.VMEM((cols, cols), F32),
            pltpu.VMEM((cols, cols), BF),
            pltpu.VMEM((cols, cols), BF),
            pltpu.VMEM((cols, cols), BF),
        ],
        compiler_params=params(32),
        name="polish",
    )(own, other, rows)


def core_swap(v):
    return lax.ppermute(v, "dp", [(i, i ^ 1) for i in range(2 * NY)])


def y_swap(v, second):
    perm = []
    for y in range(NY):
        for c in range(2):
            to = (y ^ 1) if c == second else NY - 1 - y
            perm.append((2 * y + c, 2 * to + c))
    return lax.ppermute(v, "dp", perm)


def exchange(v):
    return lax.all_to_all(v, "fsdp", split_axis=0, concat_axis=0, tiled=True)


def shards(n_rows, grads, momentum, slot_matrix):
    m = grads.shape[1]
    cols = grads.shape[3]

    send_a, send_b, keep_a, keep_b = split_rows(grads, 8)
    swapped_a = core_swap(send_a)
    swapped_b = core_swap(send_b)
    first_far = y_swap((keep_a[0].astype(F32) + swapped_a[0].astype(F32)).astype(BF), 0)
    first_own = y_swap((keep_a[1].astype(F32) + swapped_a[1].astype(F32)).astype(BF), 0)
    far = (keep_b[1].astype(F32) + swapped_b[1].astype(F32)) + first_far.astype(F32)
    second = y_swap(far.astype(BF), 1)
    parts = (slot_matrix, keep_b, swapped_b, first_own, second, momentum)
    nesterov = momentum_call(nesterov_kernel, BF, "nesterov", *parts)

    mine = exchange(nesterov)

    rows, gram_send, gram_keep = partial_gram(mine)
    gram_keep, parts = lax.optimization_barrier((gram_keep, parts))
    new_momentum = momentum_call(momentum_kernel, F32, "new_momentum", *parts)
    gram = gram_keep + core_swap(gram_send).astype(F32)
    gram = gram + y_swap(gram.astype(BF), 0).astype(F32)
    gram = gram + y_swap(gram.astype(BF), 1).astype(F32)
    own = gram.astype(BF)
    other = core_swap(own)

    update = polish(math.sqrt(max(n_rows, cols)), own, other, rows)
    return (exchange(update), new_momentum)


def solution(mesh):
    in_specs = (P("dp", None, "fsdp", None), P(None, ("fsdp", "dp"), None), P())
    out_specs = (P(None, ("fsdp", "dp"), None), P(None, ("fsdp", "dp"), None))

    def run(grads, momentum, slot_matrix):
        body = functools.partial(shards, grads.shape[2])
        return jax.shard_map(body, mesh=mesh, in_specs=in_specs, out_specs=out_specs, check_vma=False)(
            grads, momentum, slot_matrix
        )

    return run
```

```python
import functools
import math

import jax
import jax.numpy as jnp
from jax import lax
from jax.experimental import pallas as pl
from jax.experimental.pallas import tpu as pltpu
from jax.sharding import PartitionSpec as P

NY = 4
PARTS = 2
COEF_A = 3.4445
COEF_B = -4.775
COEF_C = 2.0315
DECAY = 0.95
BF = jnp.bfloat16
F32 = jnp.float32
SMEM = pltpu.SMEM


def sds(shape, dtype):
    return jax.ShapeDtypeStruct(shape, dtype)


def params(mib=16):
    return pltpu.CompilerParams(vmem_limit_bytes=mib * 1024 * 1024)


def whole(n):
    return [pl.BlockSpec(memory_space=pltpu.VMEM)] * n


def place_of():
    d = lax.axis_index("dp")
    y, c = lax.div(d, 2), lax.rem(d, 2)
    flip, turn = y + 1 - 2 * lax.rem(y, 2), NY - 1 - y
    near = jnp.where(c == 0, flip, turn)
    far = jnp.where(c == 0, turn, flip)
    return y, c, near, far, lax.rem(y + 2, NY)


def split_kernel(g_hbm, *refs):
    sends, keeps = refs[:PARTS], refs[PARTS : 2 * PARTS]
    raw, wide, sems = refs[2 * PARTS :]
    y, c, near, far, across = place_of()
    parts = sems.shape[0]
    mb = raw.shape[0] // parts

    def fetch(i):
        return pltpu.make_async_copy(
            g_hbm.at[0, pl.ds(i * mb, mb)], raw.at[pl.ds(i * mb, mb)], sems.at[i]
        )

    for i in range(parts):
        fetch(i).start()

    def emit(i, low):
        here = pl.ds(i * mb, mb)

        def fill(out, role, yy, core):
            both = wide[:, pl.ds(pl.multiple_of(8 * yy, 8), 8), :]
            chosen = both[:, 4 * core : 4 * core + 4, :].astype(BF)
            width = chosen.shape[2] // PARTS
            for p in range(PARTS):
                out[p][role, here] = chosen[:, :, width * p : width * p + width]

        for role, (mine, theirs) in enumerate(((y, y), (far, near), (across, across), (near, far))):
            fill(keeps, role, mine, low)
            fill(sends, role, theirs, 1 - low)

    for i in range(parts):
        fetch(i).wait()
        wide[...] = raw[i * mb : i * mb + mb].astype(F32)
        pl.when(c == 0)(functools.partial(emit, i, 0))
        pl.when(c == 1)(functools.partial(emit, i, 1))


def split_rows(grads, parts):
    _, m, rows, cols = grads.shape
    four = sds((4, m, 4, cols // PARTS), BF)
    return pl.pallas_call(
        split_kernel,
        in_specs=[pl.BlockSpec(memory_space=pl.ANY)],
        out_specs=whole(2 * PARTS),
        out_shape=[four] * (2 * PARTS),
        scratch_shapes=[
            pltpu.VMEM((m, rows, cols), BF),
            pltpu.VMEM((m // parts, rows, cols), F32),
            pltpu.SemaphoreType.DMA((parts,)),
        ],
        compiler_params=params(48),
        name="split_rows",
    )(grads)


def gradient_at(j, keep, swapped, first, second):
    return (keep[0, j].astype(F32) + swapped[0, j].astype(F32)) + (
        first[1, j].astype(F32) + second[j].astype(F32)
    )


def nesterov_kernel(part, slots, mom, keep, swapped, first, second, nesterov):
    m, _, width = nesterov.shape

    def step(j, carry):
        mat = slots[j]
        gradient = gradient_at(j, keep, swapped, first, second)
        old = mom[mat, :, part * width : part * width + width]
        nesterov[mat] = (gradient + DECAY * (DECAY * old + gradient)).astype(BF)
        return carry

    lax.fori_loop(0, m, step, 0, unroll=min(8, m))


def momentum_kernel(slots, mom, *refs):
    ins, new_mom = refs[:-1], refs[-1]
    m, _, cols = new_mom.shape
    width = cols // PARTS

    def step(j, carry):
        mat = slots[j]
        for p in range(PARTS):
            here = slice(p * width, p * width + width)
            new_mom[mat, :, here] = DECAY * mom[mat, :, here] + gradient_at(j, *ins[4 * p : 4 * p + 4])
        return carry

    lax.fori_loop(0, m, step, 0, unroll=min(8, m))


def momentum_call(kernel, out, name, slots, mom, *args):
    return pl.pallas_call(
        kernel,
        in_specs=[pl.BlockSpec(memory_space=SMEM)] + whole(1 + len(args)),
        out_specs=whole(1)[0],
        out_shape=out,
        compiler_params=params(),
        cost_estimate=pl.CostEstimate(flops=6 * mom.size, bytes_accessed=16 * mom.size, transcendentals=0),
        name=name,
    )(slots, mom, *args)


def blocks_of(cols):
    n = cols // 128
    return [(i, j) for i in range(n) for j in range(i, n)]


def gram_kernel(*refs):
    ins, (rows_ref, send, keep, slabs) = refs[:PARTS], refs[PARTS:]
    c = lax.rem(lax.axis_index("dp"), 2)
    cols = rows_ref.shape[1]
    count, _, width = ins[0].shape
    for p, a_ref in enumerate(ins):
        for g in range(count // 4):
            four = [a_ref[4 * g + i].astype(F32) for i in range(4)]
            rows_ref[16 * g : 16 * g + 16, p * width : p * width + width] = jnp.concatenate(four, axis=0).astype(BF)
    n = cols // 128
    b = 0
    for i in range(n):
        strip = lax.dot_general(
            rows_ref[:, 128 * i : 128 * i + 128],
            rows_ref[:, 128 * i :],
            (((0,), (0,)), ((), ())),
            preferred_element_type=F32,
        )
        for j in range(i, n):
            block = strip[:, 128 * (j - i) : 128 * (j - i) + 128]
            slabs[0, b] = block[:64, :]
            slabs[1, b] = block[64:, :]
            b += 1
    send[...] = slabs[1 - c].astype(BF)
    keep[...] = slabs[c]


def partial_gram(parts):
    count, _, width = parts[0].shape
    cols = PARTS * width
    nb = len(blocks_of(cols))
    return pl.pallas_call(
        gram_kernel,
        in_specs=whole(PARTS),
        out_specs=whole(3),
        out_shape=[
            sds((4 * count, cols), BF),
            sds((nb, 64, 128), BF),
            sds((nb, 64, 128), F32),
        ],
        scratch_shapes=[pltpu.VMEM((2, nb, 64, 128), F32)],
        compiler_params=params(),
        name="partial_gram",
    )(*parts)


def polish_kernel(scale, own, other, rows_ref, out, slabs, level, low, poly, high):
    c = lax.rem(lax.axis_index("dp"), 2)
    count, cols = rows_ref.shape
    n = cols // 128
    slabs[c] = own[...].astype(F32)
    slabs[1 - c] = other[...].astype(F32)

    eye = (
        lax.broadcasted_iota(jnp.int32, (128, 128), 0) == lax.broadcasted_iota(jnp.int32, (128, 128), 1)
    )
    diag = jnp.zeros((128, 128), F32)
    for b, (i, j) in enumerate(blocks_of(cols)):
        if i == j:
            diag += slabs[:, b].reshape(128, 128)
    trace = jnp.sum(jnp.where(eye, diag, 0.0))
    inv_norm = 1.0 / (jnp.sqrt(jnp.full((1, 1), trace)) + 1e-7)
    square = inv_norm * inv_norm
    for b, (i, j) in enumerate(blocks_of(cols)):
        block = slabs[:, b].reshape(128, 128) * square
        level[128 * i : 128 * i + 128, 128 * j : 128 * j + 128] = block
        low[128 * i : 128 * i + 128, 128 * j : 128 * j + 128] = block.astype(BF)
        if i != j:
            block = block.T
            level[128 * j : 128 * j + 128, 128 * i : 128 * i + 128] = block
            low[128 * j : 128 * j + 128, 128 * i : 128 * i + 128] = block.astype(BF)

    step = 256 if cols % 256 == 0 else 128
    for r in range(0, cols, step):
        part = jnp.dot(low[r : r + step, :], low[...], preferred_element_type=F32)
        poly[r : r + step, :] = (COEF_B * level[r : r + step, :] + COEF_C * part).astype(BF)
    for r in range(0, cols, step):
        part = jnp.dot(poly[r : r + step, :], low[...], preferred_element_type=F32)
        left_now = COEF_A * level[r : r + step, :] + part
        left_low = left_now.astype(BF)
        high[r : r + step, :] = (
            COEF_A * left_now + jnp.dot(left_low, poly[...], preferred_element_type=F32)
        ).astype(BF)
    rows = rows_ref[...]
    y0 = COEF_A * rows.astype(F32) + jnp.dot(rows, poly[...], preferred_element_type=F32)
    y1 = jnp.dot(y0.astype(BF), high[...], preferred_element_type=F32)
    y2 = jnp.dot(y1.astype(BF), high[...], preferred_element_type=F32)
    result = (COEF_A * y0 + COEF_B * y1 + COEF_C * y2) * (scale * inv_norm)
    for i in range(count // 4):
        out[i] = result[4 * i : 4 * i + 4, :].astype(BF)


def polish(scale, own, other, rows):
    count, cols = rows.shape
    nb = own.shape[0]
    return pl.pallas_call(
        functools.partial(polish_kernel, scale),
        in_specs=whole(3),
        out_specs=whole(1)[0],
        out_shape=sds((count // 4, 4, cols), BF),
        scratch_shapes=[
            pltpu.VMEM((2, nb, 64, 128), F32),
            pltpu.VMEM((cols, cols), F32),
            pltpu.VMEM((cols, cols), BF),
            pltpu.VMEM((cols, cols), BF),
            pltpu.VMEM((cols, cols), BF),
        ],
        compiler_params=params(32),
        name="polish",
    )(own, other, rows)


def core_swap(v):
    return lax.ppermute(v, "dp", [(i, i ^ 1) for i in range(2 * NY)])


def y_swap(v, second):
    perm = []
    for y in range(NY):
        for c in range(2):
            to = (y ^ 1) if c == second else NY - 1 - y
            perm.append((2 * y + c, 2 * to + c))
    return lax.ppermute(v, "dp", perm)


def exchange(v):
    return lax.all_to_all(v, "fsdp", split_axis=0, concat_axis=0, tiled=True)


def shards(n_rows, grads, momentum, slot_matrix):
    m = grads.shape[1]
    cols = grads.shape[3]

    pieces = split_rows(grads, 8)
    terms, arrived = [], []
    swaps = [core_swap(v) for v in pieces[:PARTS]]
    for p, (keep, swapped) in enumerate(zip(pieces[PARTS:], swaps)):
        first = y_swap((keep[2:].astype(F32) + swapped[2:].astype(F32)).astype(BF), 0)
        far = (keep[1].astype(F32) + swapped[1].astype(F32)) + first[0].astype(F32)
        second = y_swap(far.astype(BF), 1)
        terms += [keep, swapped, first, second]
        nesterov = momentum_call(
            functools.partial(nesterov_kernel, p),
            sds((m, 4, cols // PARTS), BF),
            "nesterov",
            slot_matrix,
            momentum,
            *terms[-4:],
        )
        arrived.append(exchange(nesterov))

    rows, gram_send, gram_keep = partial_gram(arrived)
    gram_keep, terms = lax.optimization_barrier((gram_keep, terms))
    new_momentum = momentum_call(
        momentum_kernel, sds((m, 4, cols), F32), "new_momentum", slot_matrix, momentum, *terms
    )
    gram = gram_keep + core_swap(gram_send).astype(F32)
    gram = gram + y_swap(gram.astype(BF), 0).astype(F32)
    gram = gram + y_swap(gram.astype(BF), 1).astype(F32)
    own = gram.astype(BF)
    other = core_swap(own)

    update = polish(math.sqrt(max(n_rows, cols)), own, other, rows)
    return (exchange(update), new_momentum)


def solution(mesh):
    in_specs = (P("dp", None, "fsdp", None), P(None, ("fsdp", "dp"), None), P())
    out_specs = (P(None, ("fsdp", "dp"), None), P(None, ("fsdp", "dp"), None))

    def run(grads, momentum, slot_matrix):
        body = functools.partial(shards, grads.shape[2])
        return jax.shard_map(body, mesh=mesh, in_specs=in_specs, out_specs=out_specs, check_vma=False)(
            grads, momentum, slot_matrix
        )

    return run
```

```python
import functools
import math

import jax
import jax.numpy as jnp
from jax import lax
from jax.experimental import pallas as pl
from jax.experimental.pallas import tpu as pltpu
from jax.sharding import PartitionSpec as P

NY = 4
COEF_A = 3.4445
COEF_B = -4.775
COEF_C = 2.0315
DECAY = 0.95
BF = jnp.bfloat16
F32 = jnp.float32
SMEM = pltpu.SMEM


def sds(shape, dtype):
    return jax.ShapeDtypeStruct(shape, dtype)


def params(mib=16):
    return pltpu.CompilerParams(vmem_limit_bytes=mib * 1024 * 1024)


def whole(n):
    return [pl.BlockSpec(memory_space=pltpu.VMEM)] * n


def place_of():
    d = lax.axis_index("dp")
    y, c = lax.div(d, 2), lax.rem(d, 2)
    flip, turn = y + 1 - 2 * lax.rem(y, 2), NY - 1 - y
    near = jnp.where(c == 0, flip, turn)
    far = jnp.where(c == 0, turn, flip)
    return y, c, near, far, lax.rem(y + 2, NY)


def split_kernel(g_hbm, send_a, send_b, keep_a, keep_b, raw, wide, sems):
    y, c, near, far, across = place_of()
    parts = sems.shape[0]
    mb = raw.shape[0] // parts

    def fetch(i):
        return pltpu.make_async_copy(
            g_hbm.at[0, pl.ds(i * mb, mb)], raw.at[pl.ds(i * mb, mb)], sems.at[i]
        )

    for i in range(parts):
        fetch(i).start()

    def emit(i, low):
        here = pl.ds(i * mb, mb)

        def rows(yy, core):
            both = wide[:, pl.ds(pl.multiple_of(8 * yy, 8), 8), :]
            return both[:, 4 * core : 4 * core + 4, :].astype(BF)

        send_a[0, here] = rows(across, 1 - low)
        send_a[1, here] = rows(far, 1 - low)
        send_b[0, here] = rows(y, 1 - low)
        send_b[1, here] = rows(near, 1 - low)
        keep_a[0, here] = rows(across, low)
        keep_a[1, here] = rows(near, low)
        keep_b[0, here] = rows(y, low)
        keep_b[1, here] = rows(far, low)

    for i in range(parts):
        fetch(i).wait()
        wide[...] = raw[i * mb : i * mb + mb].astype(F32)
        pl.when(c == 0)(functools.partial(emit, i, 0))
        pl.when(c == 1)(functools.partial(emit, i, 1))


def split_rows(grads, parts):
    _, m, rows, cols = grads.shape
    two = sds((2, m, 4, cols), BF)
    return pl.pallas_call(
        split_kernel,
        in_specs=[pl.BlockSpec(memory_space=pl.ANY)],
        out_specs=whole(4),
        out_shape=[two] * 4,
        scratch_shapes=[
            pltpu.VMEM((m, rows, cols), BF),
            pltpu.VMEM((m // parts, rows, cols), F32),
            pltpu.SemaphoreType.DMA((parts,)),
        ],
        compiler_params=params(48),
        name="split_rows",
    )(grads)


def gradient_at(j, keep, swapped, first, second):
    return (keep[0, j].astype(F32) + swapped[0, j].astype(F32)) + (
        first[j].astype(F32) + second[j].astype(F32)
    )


def nesterov_kernel(slots, keep, swapped, first, second, mom, nesterov):
    def step(j, carry):
        mat = slots[j]
        gradient = gradient_at(j, keep, swapped, first, second)
        nesterov[mat] = (gradient + DECAY * (DECAY * mom[mat] + gradient)).astype(BF)
        return carry

    m = mom.shape[0]
    lax.fori_loop(0, m, step, 0, unroll=min(8, m))


def momentum_kernel(slots, keep, swapped, first, second, mom, new_mom):
    def step(j, carry):
        mat = slots[j]
        new_mom[mat] = DECAY * mom[mat] + gradient_at(j, keep, swapped, first, second)
        return carry

    m = mom.shape[0]
    lax.fori_loop(0, m, step, 0, unroll=min(8, m))


def momentum_call(kernel, dtype, name, *args):
    mom = args[-1]
    return pl.pallas_call(
        kernel,
        in_specs=[pl.BlockSpec(memory_space=SMEM)] + whole(5),
        out_specs=whole(1)[0],
        out_shape=sds(mom.shape, dtype),
        compiler_params=params(),
        cost_estimate=pl.CostEstimate(flops=6 * mom.size, bytes_accessed=16 * mom.size, transcendentals=0),
        name=name,
    )(*args)


def blocks_of(cols):
    n = cols // 128
    return [(i, j) for i in range(n) for j in range(i, n)]


def gram_kernel(a_ref, rows_ref, send_a, send_b, keep_a, keep_b, slabs):
    c = lax.rem(lax.axis_index("dp"), 2)
    count, _, cols = a_ref.shape
    for g in range(count // 4):
        four = [a_ref[4 * g + i].astype(F32) for i in range(4)]
        rows_ref[16 * g : 16 * g + 16, :] = jnp.concatenate(four, axis=0).astype(BF)
    n = cols // 128
    b = 0
    for i in range(n):
        strip = lax.dot_general(
            rows_ref[:, 128 * i : 128 * i + 128],
            rows_ref[:, 128 * i :],
            (((0,), (0,)), ((), ())),
            preferred_element_type=F32,
        )
        for j in range(i, n):
            block = strip[:, 128 * (j - i) : 128 * (j - i) + 128]
            slabs[0, b] = block[:64, :]
            slabs[1, b] = block[64:, :]
            b += 1
    cut = send_a.shape[0]
    send_a[...] = slabs[1 - c, :cut].astype(BF)
    send_b[...] = slabs[1 - c, cut:].astype(BF)
    keep_a[...] = slabs[c, :cut]
    keep_b[...] = slabs[c, cut:]


def partial_gram(a):
    count, _, cols = a.shape
    nb = len(blocks_of(cols))
    halves = ((nb + 1) // 2, nb // 2)
    return pl.pallas_call(
        gram_kernel,
        in_specs=whole(1),
        out_specs=whole(5),
        out_shape=[sds((4 * count, cols), BF)] + [sds((k, 64, 128), t) for t in (BF, F32) for k in halves],
        scratch_shapes=[pltpu.VMEM((2, nb, 64, 128), F32)],
        compiler_params=params(),
        name="partial_gram",
    )(a)


def polish_kernel(scale, own_a, own_b, other_a, other_b, rows_ref, out, slabs, level, low, poly, high):
    c = lax.rem(lax.axis_index("dp"), 2)
    count, cols = rows_ref.shape
    n = cols // 128
    cut = own_a.shape[0]
    slabs[c, :cut] = own_a[...].astype(F32)
    slabs[c, cut:] = own_b[...].astype(F32)
    slabs[1 - c, :cut] = other_a[...].astype(F32)
    slabs[1 - c, cut:] = other_b[...].astype(F32)

    eye = (
        lax.broadcasted_iota(jnp.int32, (128, 128), 0) == lax.broadcasted_iota(jnp.int32, (128, 128), 1)
    )
    diag = jnp.zeros((128, 128), F32)
    for b, (i, j) in enumerate(blocks_of(cols)):
        if i == j:
            diag += slabs[:, b].reshape(128, 128)
    trace = jnp.sum(jnp.where(eye, diag, 0.0))
    inv_norm = 1.0 / (jnp.sqrt(jnp.full((1, 1), trace)) + 1e-7)
    square = inv_norm * inv_norm
    for b, (i, j) in enumerate(blocks_of(cols)):
        block = slabs[:, b].reshape(128, 128) * square
        level[128 * i : 128 * i + 128, 128 * j : 128 * j + 128] = block
        low[128 * i : 128 * i + 128, 128 * j : 128 * j + 128] = block.astype(BF)
        if i != j:
            block = block.T
            level[128 * j : 128 * j + 128, 128 * i : 128 * i + 128] = block
            low[128 * j : 128 * j + 128, 128 * i : 128 * i + 128] = block.astype(BF)

    step = 256 if cols % 256 == 0 else 128
    for r in range(0, cols, step):
        part = jnp.dot(low[r : r + step, :], low[...], preferred_element_type=F32)
        poly[r : r + step, :] = (COEF_B * level[r : r + step, :] + COEF_C * part).astype(BF)
    for r in range(0, cols, step):
        part = jnp.dot(poly[r : r + step, :], low[...], preferred_element_type=F32)
        left_now = COEF_A * level[r : r + step, :] + part
        left_low = left_now.astype(BF)
        high[r : r + step, :] = (
            COEF_A * left_now + jnp.dot(left_low, poly[...], preferred_element_type=F32)
        ).astype(BF)
    rows = rows_ref[...]
    y0 = COEF_A * rows.astype(F32) + jnp.dot(rows, poly[...], preferred_element_type=F32)
    y1 = jnp.dot(y0.astype(BF), high[...], preferred_element_type=F32)
    y2 = jnp.dot(y1.astype(BF), high[...], preferred_element_type=F32)
    result = (COEF_A * y0 + COEF_B * y1 + COEF_C * y2) * (scale * inv_norm)
    for i in range(count // 4):
        out[i] = result[4 * i : 4 * i + 4, :].astype(BF)


def polish(scale, own, other, rows):
    count, cols = rows.shape
    nb = sum(v.shape[0] for v in own)
    return pl.pallas_call(
        functools.partial(polish_kernel, scale),
        in_specs=whole(5),
        out_specs=whole(1)[0],
        out_shape=sds((count // 4, 4, cols), BF),
        scratch_shapes=[
            pltpu.VMEM((2, nb, 64, 128), F32),
            pltpu.VMEM((cols, cols), F32),
            pltpu.VMEM((cols, cols), BF),
            pltpu.VMEM((cols, cols), BF),
            pltpu.VMEM((cols, cols), BF),
        ],
        compiler_params=params(32),
        name="polish",
    )(*own, *other, rows)


def core_swap(v):
    return lax.ppermute(v, "dp", [(i, i ^ 1) for i in range(2 * NY)])


def y_swap(v, second):
    perm = []
    for y in range(NY):
        for c in range(2):
            to = (y ^ 1) if c == second else NY - 1 - y
            perm.append((2 * y + c, 2 * to + c))
    return lax.ppermute(v, "dp", perm)


def exchange(v):
    return lax.all_to_all(v, "fsdp", split_axis=0, concat_axis=0, tiled=True)


def shards(n_rows, grads, momentum, slot_matrix):
    m = grads.shape[1]
    cols = grads.shape[3]

    send_a, send_b, keep_a, keep_b = split_rows(grads, 8)
    swapped_a = core_swap(send_a)
    swapped_b = core_swap(send_b)
    first_far = y_swap((keep_a[0].astype(F32) + swapped_a[0].astype(F32)).astype(BF), 0)
    first_own = y_swap((keep_a[1].astype(F32) + swapped_a[1].astype(F32)).astype(BF), 0)
    far = (keep_b[1].astype(F32) + swapped_b[1].astype(F32)) + first_far.astype(F32)
    second = y_swap(far.astype(BF), 1)
    parts = (slot_matrix, keep_b, swapped_b, first_own, second, momentum)
    nesterov = momentum_call(nesterov_kernel, BF, "nesterov", *parts)

    mine = exchange(nesterov)

    rows, *pieces = partial_gram(mine)
    sends, keeps = pieces[:2], pieces[2:]
    keeps, parts = lax.optimization_barrier((keeps, parts))
    new_momentum = momentum_call(momentum_kernel, F32, "new_momentum", *parts)
    grams = [keep + core_swap(send).astype(F32) for keep, send in zip(keeps, sends)]
    grams = [gram + y_swap(gram.astype(BF), 0).astype(F32) for gram in grams]
    grams = [gram + y_swap(gram.astype(BF), 1).astype(F32) for gram in grams]
    own = [gram.astype(BF) for gram in grams]
    other = [core_swap(gram) for gram in own]

    update = polish(math.sqrt(max(n_rows, cols)), own, other, rows)
    return (exchange(update), new_momentum)


def solution(mesh):
    in_specs = (P("dp", None, "fsdp", None), P(None, ("fsdp", "dp"), None), P())
    out_specs = (P(None, ("fsdp", "dp"), None), P(None, ("fsdp", "dp"), None))

    def run(grads, momentum, slot_matrix):
        body = functools.partial(shards, grads.shape[2])
        return jax.shard_map(body, mesh=mesh, in_specs=in_specs, out_specs=out_specs, check_vma=False)(
            grads, momentum, slot_matrix
        )

    return run
```

```python
import functools
import math

import jax
import jax.numpy as jnp
from jax import lax
from jax.experimental import pallas as pl
from jax.experimental.pallas import tpu as pltpu
from jax.sharding import PartitionSpec as P

NY = 4
COEF_A = 3.4445
COEF_B = -4.775
COEF_C = 2.0315
DECAY = 0.95
BF = jnp.bfloat16
F32 = jnp.float32
SMEM = pltpu.SMEM


def sds(shape, dtype):
    return jax.ShapeDtypeStruct(shape, dtype)


def params(mib=16):
    return pltpu.CompilerParams(vmem_limit_bytes=mib * 1024 * 1024)


def whole(n):
    return [pl.BlockSpec(memory_space=pltpu.VMEM)] * n


def place_of():
    d = lax.axis_index("dp")
    y, c = lax.div(d, 2), lax.rem(d, 2)
    flip, turn = y + 1 - 2 * lax.rem(y, 2), NY - 1 - y
    near = jnp.where(c == 0, flip, turn)
    far = jnp.where(c == 0, turn, flip)
    return y, c, near, far, lax.rem(y + 2, NY)


def split_kernel(g_hbm, send_a, send_b, keep_a, keep_b, raw, wide, sems):
    y, c, near, far, across = place_of()
    parts = sems.shape[0]
    mb = raw.shape[0] // parts

    def fetch(i):
        return pltpu.make_async_copy(
            g_hbm.at[0, pl.ds(i * mb, mb)], raw.at[pl.ds(i * mb, mb)], sems.at[i]
        )

    for i in range(parts):
        fetch(i).start()

    def emit(i, low):
        here = pl.ds(i * mb, mb)

        def rows(yy, core):
            both = wide[:, pl.ds(pl.multiple_of(8 * yy, 8), 8), :]
            return both[:, 4 * core : 4 * core + 4, :].astype(BF)

        send_a[0, here] = rows(across, 1 - low)
        send_a[1, here] = rows(far, 1 - low)
        send_b[0, here] = rows(y, 1 - low)
        send_b[1, here] = rows(near, 1 - low)
        keep_a[0, here] = rows(across, low)
        keep_a[1, here] = rows(near, low)
        keep_b[0, here] = rows(y, low)
        keep_b[1, here] = rows(far, low)

    for i in range(parts):
        fetch(i).wait()
        wide[...] = raw[i * mb : i * mb + mb].astype(F32)
        pl.when(c == 0)(functools.partial(emit, i, 0))
        pl.when(c == 1)(functools.partial(emit, i, 1))


def split_rows(grads, parts):
    _, m, rows, cols = grads.shape
    two = sds((2, m, 4, cols), BF)
    return pl.pallas_call(
        split_kernel,
        in_specs=[pl.BlockSpec(memory_space=pl.ANY)],
        out_specs=whole(4),
        out_shape=[two] * 4,
        scratch_shapes=[
            pltpu.VMEM((m, rows, cols), BF),
            pltpu.VMEM((m // parts, rows, cols), F32),
            pltpu.SemaphoreType.DMA((parts,)),
        ],
        compiler_params=params(48),
        name="split_rows",
    )(grads)


def gradient_at(j, keep, swapped, first, second):
    return (keep[0, j].astype(F32) + swapped[0, j].astype(F32)) + (
        first[j].astype(F32) + second[j].astype(F32)
    )


def nesterov_kernel(slots, keep, swapped, first, second, mom, nesterov):
    def step(j, carry):
        mat = slots[j]
        gradient = gradient_at(j, keep, swapped, first, second)
        nesterov[mat] = (gradient + DECAY * (DECAY * mom[mat] + gradient)).astype(BF)
        return carry

    m = mom.shape[0]
    lax.fori_loop(0, m, step, 0, unroll=min(8, m))


def momentum_kernel(slots, keep, swapped, first, second, mom, new_mom):
    def step(j, carry):
        mat = slots[j]
        new_mom[mat] = DECAY * mom[mat] + gradient_at(j, keep, swapped, first, second)
        return carry

    m = mom.shape[0]
    lax.fori_loop(0, m, step, 0, unroll=min(8, m))


def momentum_call(kernel, dtype, name, *args):
    mom = args[-1]
    return pl.pallas_call(
        kernel,
        in_specs=[pl.BlockSpec(memory_space=SMEM)] + whole(5),
        out_specs=whole(1)[0],
        out_shape=sds(mom.shape, dtype),
        compiler_params=params(),
        cost_estimate=pl.CostEstimate(flops=6 * mom.size, bytes_accessed=16 * mom.size, transcendentals=0),
        name=name,
    )(*args)


def blocks_of(cols):
    n = cols // 128
    return [(i, j) for i in range(n) for j in range(i, n)]


def gram_kernel(a_ref, rows_ref, send, keep, slabs):
    c = lax.rem(lax.axis_index("dp"), 2)
    count, _, cols = a_ref.shape
    for g in range(count // 4):
        four = [a_ref[4 * g + i].astype(F32) for i in range(4)]
        rows_ref[16 * g : 16 * g + 16, :] = jnp.concatenate(four, axis=0).astype(BF)
    n = cols // 128
    b = 0
    for i in range(n):
        strip = lax.dot_general(
            rows_ref[:, 128 * i : 128 * i + 128],
            rows_ref[:, 128 * i :],
            (((0,), (0,)), ((), ())),
            preferred_element_type=F32,
        )
        for j in range(i, n):
            block = strip[:, 128 * (j - i) : 128 * (j - i) + 128]
            slabs[0, b] = block[:64, :]
            slabs[1, b] = block[64:, :]
            b += 1
    send[...] = slabs[1 - c].astype(BF)
    keep[...] = slabs[c]


def partial_gram(a):
    count, _, cols = a.shape
    nb = len(blocks_of(cols))
    return pl.pallas_call(
        gram_kernel,
        in_specs=whole(1),
        out_specs=whole(3),
        out_shape=[
            sds((4 * count, cols), BF),
            sds((nb, 64, 128), BF),
            sds((nb, 64, 128), F32),
        ],
        scratch_shapes=[pltpu.VMEM((2, nb, 64, 128), F32)],
        compiler_params=params(),
        name="partial_gram",
    )(a)


def polish_kernel(scale, own, other, rows_ref, out, slabs, level, low, poly, high):
    c = lax.rem(lax.axis_index("dp"), 2)
    count, cols = rows_ref.shape
    n = cols // 128
    slabs[c] = own[...].astype(F32)
    slabs[1 - c] = other[...].astype(F32)

    eye = (
        lax.broadcasted_iota(jnp.int32, (128, 128), 0) == lax.broadcasted_iota(jnp.int32, (128, 128), 1)
    )
    diag = jnp.zeros((128, 128), F32)
    for b, (i, j) in enumerate(blocks_of(cols)):
        if i == j:
            diag += slabs[:, b].reshape(128, 128)
    trace = jnp.sum(jnp.where(eye, diag, 0.0))
    inv_norm = 1.0 / (jnp.sqrt(jnp.full((1, 1), trace)) + 1e-7)
    square = inv_norm * inv_norm
    for b, (i, j) in enumerate(blocks_of(cols)):
        block = slabs[:, b].reshape(128, 128) * square
        level[128 * i : 128 * i + 128, 128 * j : 128 * j + 128] = block
        low[128 * i : 128 * i + 128, 128 * j : 128 * j + 128] = block.astype(BF)
        if i != j:
            block = block.T
            level[128 * j : 128 * j + 128, 128 * i : 128 * i + 128] = block
            low[128 * j : 128 * j + 128, 128 * i : 128 * i + 128] = block.astype(BF)

    step = 256 if cols % 256 == 0 else 128
    for r in range(0, cols, step):
        part = jnp.dot(low[r : r + step, :], low[...], preferred_element_type=F32)
        poly[r : r + step, :] = (COEF_B * level[r : r + step, :] + COEF_C * part).astype(BF)
    for r in range(0, cols, step):
        part = jnp.dot(poly[r : r + step, :], low[...], preferred_element_type=F32)
        left_now = COEF_A * level[r : r + step, :] + part
        left_low = left_now.astype(BF)
        high[r : r + step, :] = (
            COEF_A * left_now + jnp.dot(left_low, poly[...], preferred_element_type=F32)
        ).astype(BF)
    rows = rows_ref[...]
    y0 = COEF_A * rows.astype(F32) + jnp.dot(rows, poly[...], preferred_element_type=F32)
    y1 = jnp.dot(y0.astype(BF), high[...], preferred_element_type=F32)
    y2 = jnp.dot(y1.astype(BF), high[...], preferred_element_type=F32)
    result = (COEF_A * y0 + COEF_B * y1 + COEF_C * y2) * (scale * inv_norm)
    for i in range(count // 4):
        out[i] = result[4 * i : 4 * i + 4, :].astype(BF)


def polish(scale, own, other, rows):
    count, cols = rows.shape
    nb = own.shape[0]
    return pl.pallas_call(
        functools.partial(polish_kernel, scale),
        in_specs=whole(3),
        out_specs=whole(1)[0],
        out_shape=sds((count // 4, 4, cols), BF),
        scratch_shapes=[
            pltpu.VMEM((2, nb, 64, 128), F32),
            pltpu.VMEM((cols, cols), F32),
            pltpu.VMEM((cols, cols), BF),
            pltpu.VMEM((cols, cols), BF),
            pltpu.VMEM((cols, cols), BF),
        ],
        compiler_params=params(32),
        name="polish",
    )(own, other, rows)


def core_swap(v):
    return lax.ppermute(v, "dp", [(i, i ^ 1) for i in range(2 * NY)])


def y_swap(v, second):
    perm = []
    for y in range(NY):
        for c in range(2):
            to = (y ^ 1) if c == second else NY - 1 - y
            perm.append((2 * y + c, 2 * to + c))
    return lax.ppermute(v, "dp", perm)


def exchange(v):
    return lax.all_to_all(v, "fsdp", split_axis=0, concat_axis=0, tiled=True)


def shards(n_rows, grads, momentum, slot_matrix):
    m = grads.shape[1]
    cols = grads.shape[3]

    send_a, send_b, keep_a, keep_b = split_rows(grads, 8)
    swapped_a = core_swap(send_a)
    swapped_b = core_swap(send_b)
    first_far = y_swap((keep_a[0].astype(F32) + swapped_a[0].astype(F32)).astype(BF), 0)
    first_own = y_swap((keep_a[1].astype(F32) + swapped_a[1].astype(F32)).astype(BF), 0)
    far = (keep_b[1].astype(F32) + swapped_b[1].astype(F32)) + first_far.astype(F32)
    second = y_swap(far.astype(BF), 1)
    parts = (slot_matrix, keep_b, swapped_b, first_own, second, momentum)
    nesterov = momentum_call(nesterov_kernel, BF, "nesterov", *parts)

    mine = exchange(nesterov)

    rows, gram_send, gram_keep = partial_gram(mine)
    gram_keep, parts = lax.optimization_barrier((gram_keep, parts))
    new_momentum = momentum_call(momentum_kernel, F32, "new_momentum", *parts)
    gram = gram_keep + core_swap(gram_send).astype(F32)
    gram = gram + y_swap(gram.astype(BF), 0).astype(F32)
    gram = gram + y_swap(gram.astype(BF), 1).astype(F32)
    own = gram.astype(BF)
    other, new_momentum = lax.optimization_barrier((core_swap(own), new_momentum))

    update = polish(math.sqrt(max(n_rows, cols)), own, other, rows)
    return (exchange(update), new_momentum)


def solution(mesh):
    in_specs = (P("dp", None, "fsdp", None), P(None, ("fsdp", "dp"), None), P())
    out_specs = (P(None, ("fsdp", "dp"), None), P(None, ("fsdp", "dp"), None))

    def run(grads, momentum, slot_matrix):
        body = functools.partial(shards, grads.shape[2])
        return jax.shard_map(body, mesh=mesh, in_specs=in_specs, out_specs=out_specs, check_vma=False)(
            grads, momentum, slot_matrix
        )

    return run
```

```python
import functools
import math

import jax
import jax.numpy as jnp
from jax import lax
from jax.experimental import pallas as pl
from jax.experimental.pallas import tpu as pltpu
from jax.sharding import PartitionSpec as P

NY = 4
COEF_A = 3.4445
COEF_B = -4.775
COEF_C = 2.0315
DECAY = 0.95
BF = jnp.bfloat16
F32 = jnp.float32
SMEM = pltpu.SMEM


def sds(shape, dtype):
    return jax.ShapeDtypeStruct(shape, dtype)


def params(mib=16):
    return pltpu.CompilerParams(vmem_limit_bytes=mib * 1024 * 1024)


def whole(n):
    return [pl.BlockSpec(memory_space=pltpu.VMEM)] * n


def place_of():
    d = lax.axis_index("dp")
    y, c = lax.div(d, 2), lax.rem(d, 2)
    flip, turn = y + 1 - 2 * lax.rem(y, 2), NY - 1 - y
    near = jnp.where(c == 0, flip, turn)
    far = jnp.where(c == 0, turn, flip)
    return y, c, near, far, lax.rem(y + 2, NY)


def split_kernel(g_hbm, send_a, send_b, keep_a, keep_b, raw, wide, sems):
    y, c, near, far, across = place_of()
    parts = sems.shape[0]
    mb = raw.shape[0] // parts

    def fetch(i):
        return pltpu.make_async_copy(
            g_hbm.at[0, pl.ds(i * mb, mb)], raw.at[pl.ds(i * mb, mb)], sems.at[i]
        )

    for i in range(parts):
        fetch(i).start()

    def emit(i, low):
        here = pl.ds(i * mb, mb)

        def rows(yy, core):
            both = wide[:, pl.ds(pl.multiple_of(8 * yy, 8), 8), :]
            return both[:, 4 * core : 4 * core + 4, :].astype(BF)

        send_a[0, here] = rows(across, 1 - low)
        send_a[1, here] = rows(far, 1 - low)
        send_b[0, here] = rows(y, 1 - low)
        send_b[1, here] = rows(near, 1 - low)
        keep_a[0, here] = rows(across, low)
        keep_a[1, here] = rows(near, low)
        keep_b[0, here] = rows(y, low)
        keep_b[1, here] = rows(far, low)

    for i in range(parts):
        fetch(i).wait()
        wide[...] = raw[i * mb : i * mb + mb].astype(F32)
        pl.when(c == 0)(functools.partial(emit, i, 0))
        pl.when(c == 1)(functools.partial(emit, i, 1))


def split_rows(grads, parts):
    _, m, rows, cols = grads.shape
    two = sds((2, m, 4, cols), BF)
    return pl.pallas_call(
        split_kernel,
        in_specs=[pl.BlockSpec(memory_space=pl.ANY)],
        out_specs=whole(4),
        out_shape=[two] * 4,
        scratch_shapes=[
            pltpu.VMEM((m, rows, cols), BF),
            pltpu.VMEM((m // parts, rows, cols), F32),
            pltpu.SemaphoreType.DMA((parts,)),
        ],
        compiler_params=params(48),
        name="split_rows",
    )(grads)


def gradient_at(j, keep, swapped, first, second):
    return (keep[0, j].astype(F32) + swapped[0, j].astype(F32)) + (
        first[j].astype(F32) + second[j].astype(F32)
    )


def nesterov_kernel(slots, keep, swapped, first, second, mom, nesterov):
    def step(j, carry):
        mat = slots[j]
        gradient = gradient_at(j, keep, swapped, first, second)
        nesterov[mat] = (gradient + DECAY * (DECAY * mom[mat] + gradient)).astype(BF)
        return carry

    m = mom.shape[0]
    lax.fori_loop(0, m, step, 0, unroll=min(8, m))


def momentum_kernel(slots, keep, swapped, first, second, mom, new_mom):
    def step(j, carry):
        mat = slots[j]
        new_mom[mat] = DECAY * mom[mat] + gradient_at(j, keep, swapped, first, second)
        return carry

    m = mom.shape[0]
    lax.fori_loop(0, m, step, 0, unroll=min(8, m))


def momentum_call(kernel, dtype, name, *args):
    mom = args[-1]
    return pl.pallas_call(
        kernel,
        in_specs=[pl.BlockSpec(memory_space=SMEM)] + whole(5),
        out_specs=whole(1)[0],
        out_shape=sds(mom.shape, dtype),
        compiler_params=params(),
        cost_estimate=pl.CostEstimate(flops=6 * mom.size, bytes_accessed=16 * mom.size, transcendentals=0),
        name=name,
    )(*args)


def blocks_of(cols):
    n = cols // 128
    return [(i, j) for i in range(n) for j in range(i, n)]


def gram_kernel(a_ref, rows_ref, send, keep, slabs):
    c = lax.rem(lax.axis_index("dp"), 2)
    count, _, cols = a_ref.shape
    for g in range(count // 4):
        four = [a_ref[4 * g + i].astype(F32) for i in range(4)]
        rows_ref[16 * g : 16 * g + 16, :] = jnp.concatenate(four, axis=0).astype(BF)
    n = cols // 128
    b = 0
    for i in range(n):
        strip = lax.dot_general(
            rows_ref[:, 128 * i : 128 * i + 128],
            rows_ref[:, 128 * i :],
            (((0,), (0,)), ((), ())),
            preferred_element_type=F32,
        )
        for j in range(i, n):
            block = strip[:, 128 * (j - i) : 128 * (j - i) + 128]
            slabs[0, b] = block[:64, :]
            slabs[1, b] = block[64:, :]
            b += 1
    send[...] = slabs[1 - c].astype(BF)
    keep[...] = slabs[c]


def partial_gram(a):
    count, _, cols = a.shape
    nb = len(blocks_of(cols))
    return pl.pallas_call(
        gram_kernel,
        in_specs=whole(1),
        out_specs=whole(3),
        out_shape=[
            sds((4 * count, cols), BF),
            sds((nb, 64, 128), BF),
            sds((nb, 64, 128), F32),
        ],
        scratch_shapes=[pltpu.VMEM((2, nb, 64, 128), F32)],
        compiler_params=params(),
        name="partial_gram",
    )(a)


def polish_kernel(scale, own, other, rows_ref, out, slabs, level, low, poly, high):
    c = lax.rem(lax.axis_index("dp"), 2)
    count, cols = rows_ref.shape
    n = cols // 128
    slabs[c] = own[...].astype(F32)
    slabs[1 - c] = other[...].astype(F32)

    eye = (
        lax.broadcasted_iota(jnp.int32, (128, 128), 0) == lax.broadcasted_iota(jnp.int32, (128, 128), 1)
    )
    diag = jnp.zeros((128, 128), F32)
    for b, (i, j) in enumerate(blocks_of(cols)):
        if i == j:
            diag += slabs[:, b].reshape(128, 128)
    trace = jnp.sum(jnp.where(eye, diag, 0.0))
    inv_norm = 1.0 / (jnp.sqrt(jnp.full((1, 1), trace)) + 1e-7)
    square = inv_norm * inv_norm
    for b, (i, j) in enumerate(blocks_of(cols)):
        block = slabs[:, b].reshape(128, 128) * square
        level[128 * i : 128 * i + 128, 128 * j : 128 * j + 128] = block
        low[128 * i : 128 * i + 128, 128 * j : 128 * j + 128] = block.astype(BF)
        if i != j:
            block = block.T
            level[128 * j : 128 * j + 128, 128 * i : 128 * i + 128] = block
            low[128 * j : 128 * j + 128, 128 * i : 128 * i + 128] = block.astype(BF)

    step = 256 if cols % 256 == 0 else 128
    for r in range(0, cols, step):
        part = jnp.dot(low[r : r + step, :], low[...], preferred_element_type=F32)
        poly[r : r + step, :] = (COEF_B * level[r : r + step, :] + COEF_C * part).astype(BF)
    for r in range(0, cols, step):
        part = jnp.dot(poly[r : r + step, :], low[...], preferred_element_type=F32)
        left_now = COEF_A * level[r : r + step, :] + part
        left_low = left_now.astype(BF)
        high[r : r + step, :] = (
            COEF_A * left_now + jnp.dot(left_low, poly[...], preferred_element_type=F32)
        ).astype(BF)
    rows = rows_ref[...]
    y0 = COEF_A * rows.astype(F32) + jnp.dot(rows, poly[...], preferred_element_type=F32)
    y1 = jnp.dot(y0.astype(BF), high[...], preferred_element_type=F32)
    y2 = jnp.dot(y1.astype(BF), high[...], preferred_element_type=F32)
    result = (COEF_A * y0 + COEF_B * y1 + COEF_C * y2) * (scale * inv_norm)
    for i in range(count // 4):
        out[i] = result[4 * i : 4 * i + 4, :].astype(BF)


def polish(scale, own, other, rows):
    count, cols = rows.shape
    nb = own.shape[0]
    return pl.pallas_call(
        functools.partial(polish_kernel, scale),
        in_specs=whole(3),
        out_specs=whole(1)[0],
        out_shape=sds((count // 4, 4, cols), BF),
        scratch_shapes=[
            pltpu.VMEM((2, nb, 64, 128), F32),
            pltpu.VMEM((cols, cols), F32),
            pltpu.VMEM((cols, cols), BF),
            pltpu.VMEM((cols, cols), BF),
            pltpu.VMEM((cols, cols), BF),
        ],
        compiler_params=params(32),
        name="polish",
    )(own, other, rows)


def core_swap(v):
    return lax.ppermute(v, "dp", [(i, i ^ 1) for i in range(2 * NY)])


def y_swap(v, second):
    perm = []
    for y in range(NY):
        for c in range(2):
            to = (y ^ 1) if c == second else NY - 1 - y
            perm.append((2 * y + c, 2 * to + c))
    return lax.ppermute(v, "dp", perm)


def y_cross(v):
    perm = []
    for y in range(NY):
        perm += [(2 * y, 2 * (NY - 1 - y) + 1), (2 * y + 1, 2 * (y ^ 1))]
    return lax.ppermute(v, "dp", perm)


def exchange(v):
    return lax.all_to_all(v, "fsdp", split_axis=0, concat_axis=0, tiled=True)


def shards(n_rows, grads, momentum, slot_matrix):
    m = grads.shape[1]
    cols = grads.shape[3]

    send_a, send_b, keep_a, keep_b = split_rows(grads, 8)
    swapped_a = core_swap(send_a)
    swapped_b = core_swap(send_b)
    first_far = y_swap((keep_a[0].astype(F32) + swapped_a[0].astype(F32)).astype(BF), 0)
    first_own = y_swap((keep_a[1].astype(F32) + swapped_a[1].astype(F32)).astype(BF), 0)
    far = (keep_b[1].astype(F32) + swapped_b[1].astype(F32)) + first_far.astype(F32)
    second = y_swap(far.astype(BF), 1)
    parts = (slot_matrix, keep_b, swapped_b, first_own, second, momentum)
    nesterov = momentum_call(nesterov_kernel, BF, "nesterov", *parts)

    mine = exchange(nesterov)

    rows, gram_send, gram_keep = partial_gram(mine)
    gram_keep, parts = lax.optimization_barrier((gram_keep, parts))
    new_momentum = momentum_call(momentum_kernel, F32, "new_momentum", *parts)
    gram = gram_keep + core_swap(gram_send).astype(F32)
    gram = gram + y_swap(gram.astype(BF), 0).astype(F32)
    low = gram.astype(BF)
    other = (core_swap(low).astype(F32) + y_cross(low).astype(F32)).astype(BF)
    own = (low.astype(F32) + y_swap(low, 1).astype(F32)).astype(BF)
    other, new_momentum = lax.optimization_barrier((other, new_momentum))

    update = polish(math.sqrt(max(n_rows, cols)), own, other, rows)
    return (exchange(update), new_momentum)


def solution(mesh):
    in_specs = (P("dp", None, "fsdp", None), P(None, ("fsdp", "dp"), None), P())
    out_specs = (P(None, ("fsdp", "dp"), None), P(None, ("fsdp", "dp"), None))

    def run(grads, momentum, slot_matrix):
        body = functools.partial(shards, grads.shape[2])
        return jax.shard_map(body, mesh=mesh, in_specs=in_specs, out_specs=out_specs, check_vma=False)(
            grads, momentum, slot_matrix
        )

    return run
```
